512 devices in a mesh: pair: 64 (over x, z), virt: 8 (over y, core).
Axes of the slice: x: 4, y: 4, z: 16, core: 2. Of those that a mesh axis runs over, the one named last changes fastest.
Arguments:
- amplitudes: bfloat16 [2, 64, 1024, 1024], P(None, 'pair', None, 'virt'), may hold values from -8.5 to 8.5, as said below
- w_ovvo: bfloat16 [64, 1024, 1024], P('pair', 'virt'), may hold values from -0.09375 to 0.09375
- occ_irreps: int32 [8], replicated, may hold values from 0 to 7
- vir_irreps: int32 [1024], replicated, may hold values from 0 to 7, as said below
Outputs:
- sigma_cycle: bfloat16 [2, 64, 1024, 1024], P(None, 'pair', None, 'virt')
The draws below stay inside these ranges and needn't reach their ends.
Inputs may be any that keep to these rules, and one draw needn't show every extreme that they name: amplitudes[x, i*8+j, a, b] equals amplitudes[x, j*8+i, b, a] exactly. `vir_irreps`: non-decreasing along the orbitals, so each irrep is one contiguous block; the first entry is 0 and the last 7.
All inputs are finite; a program needn't handle non-finite values.
Results may differ from the reference program's by a relative error of at most 0.017.
Values may be sent and summed in bfloat16 or wider, within the bound.
A program may use at most 64 MiB of HBM per device.

```python
import jax
import jax.numpy as jnp
from jax import lax

V = 1024
NVEC = 2
O = 8
PAIRS = 64
N_VIRT = 8


def draw_amplitudes(key, part):
    key = jax.random.fold_in(key, 11)
    base = jnp.clip(jax.random.normal(key, (NVEC, O, O, V, V), jnp.float32), -6.0, 6.0)
    paired = (base + jnp.transpose(base, (0, 2, 1, 4, 3))) * 0.70710678
    return paired.reshape(NVEC, O * O, V, V).astype(jnp.bfloat16)


def draw_vir_irreps(key, part):
    key = jax.random.fold_in(key, 23)
    scores = jax.random.randint(key, (V,), 0, 36)
    scores = scores.at[0].set(0).at[V - 1].set(35)
    thresholds = jnp.array([8, 15, 21, 26, 30, 33, 35], jnp.int32)
    labels = jnp.sum((scores[:, None] >= thresholds[None, :]).astype(jnp.int32), axis=1)
    return jnp.sort(labels).astype(jnp.int32)


def set_ends(values, rng, low, top_value):
    spot = [jax.random.randint(jax.random.fold_in(rng, axis), (), 0, length) for axis, length in enumerate(values.shape)]
    longest = values.shape.index(max(values.shape))
    beside = spot[:longest] + [(spot[longest] + 1) % values.shape[longest]] + spot[longest + 1:]
    return values.at[tuple(spot)].set(low).at[tuple(beside)].set(top_value)


def spiked(values, own_key, source, target, parts, factor):
    def block_of(axis_at):
        return (jnp.arange(values.shape[axis_at]) // (values.shape[axis_at] // parts)).reshape((-1,) + (1,) * (values.ndim - 1 - axis_at))

    near = jax.random.permutation(own_key, parts)[block_of(target)]
    second = (block_of(target) + parts // 2) % parts
    return jnp.where((block_of(source) == near) | (block_of(source) == second), factor * values, values)


def block_scale(rng, dims, cuts, least, high):
    def one(dim, blocks):
        draws = jax.random.uniform(jax.random.fold_in(jax.random.fold_in(rng, 6), dim), (blocks,), jnp.float32, least / len(cuts), high / len(cuts))
        return jnp.repeat(jnp.exp(draws), dims[dim] // blocks).reshape((-1,) + (1,) * (len(dims) - dim - 1))

    factor_of = one(*cuts[0])
    for cut in cuts[1:]:
        factor_of = factor_of * one(*cut)
    return factor_of


def gaussian_with(key, dims, width, reach, split, heavy, kind=jnp.bfloat16):
    values = width * jax.random.normal(key, dims, jnp.float32)
    if split:
        values = values * block_scale(key, dims, split, -0.22, 0.18)
    return jnp.clip(spiked(values, jax.random.fold_in(key, 3), *heavy), -reach, reach).astype(kind)


def setup_inputs(seed: int = 0) -> dict:
    streams_of = jax.random.split(jax.random.key(seed), 5)
    return {
        "amplitudes": draw_amplitudes(jax.random.fold_in(streams_of[4], 71), 0),
        "w_ovvo": gaussian_with(streams_of[1], (PAIRS, V, V), (O * V) ** -0.5, 0.09375, ((0, 64), (1, 8)), (1, 2, 8, 2.0)),
        "occ_irreps": set_ends(jax.random.randint(streams_of[2], (O,), 0, 8), jax.random.fold_in(streams_of[2], 1), 0, 7).astype(jnp.int32),
        "vir_irreps": draw_vir_irreps(jax.random.fold_in(streams_of[4], 71), 0),
    }


def reference(amplitudes, w_ovvo, occ_irreps, vir_irreps):
    widened = amplitudes.astype(jnp.float32).reshape(NVEC, O, O, V, V)
    cycle_all = (2.0 * widened - jnp.transpose(widened, (0, 2, 1, 3, 4))).astype(jnp.bfloat16)
    cycle_all = lax.optimization_barrier(cycle_all)
    weights = w_ovvo.reshape(O, O, V, V)
    block_cols = V // N_VIRT
    vir_product = jnp.bitwise_xor(vir_irreps[:, None], vir_irreps[None, :])

    def one_pair(index):
        left_occ = index // O
        right_occ = index % O
        cycle_rows = lax.dynamic_index_in_dim(cycle_all, left_occ, 1, keepdims=False)
        weight_cols = lax.dynamic_index_in_dim(weights, right_occ, 1, keepdims=False)
        cycle_rows = cycle_rows.reshape(NVEC, O, V, N_VIRT, block_cols).astype(jnp.float32)
        weight_cols = weight_cols.reshape(O, N_VIRT, block_cols, V).astype(jnp.float32)
        partial_value = jnp.einsum("xkavc,kvcb->vxab", cycle_rows, weight_cols)
        rounded = lax.optimization_barrier(partial_value.astype(jnp.bfloat16))
        summed = jnp.sum(rounded.astype(jnp.float32), axis=0)
        target = jnp.bitwise_xor(occ_irreps[left_occ], occ_irreps[right_occ])
        allowed = vir_product == target
        return jnp.where(allowed[None], summed, 0.0).astype(jnp.bfloat16)

    result = lax.map(one_pair, jnp.arange(O * O, dtype=jnp.int32))
    return jnp.transpose(result, (1, 0, 2, 3))
```

```python
import functools
import math

import jax
import jax.numpy as jnp
from jax import lax
from jax.experimental import pallas as pl
from jax.experimental.pallas import tpu as pltpu
from jax.sharding import PartitionSpec as P

MESH = pl.DeviceIdType.MESH
BF = jnp.bfloat16
F32 = jnp.float32

NX, NZ, NY = 4, 16, 4
O = 8
NV = 8
V = 1024
BV = 128
CAP = 288


def swapped(block, axis, stride):
    count = lax.axis_size(axis)
    route = []
    for low in range(count):
        high = low | 1 << stride
        if high != low and high < count:
            route += [(low, high), (high, low)]
    return lax.ppermute(block, axis, route)


def bit_of(position, level):
    return position // 2**level % 2


def general(amplitudes, w_ovvo, occ_irreps, vir_irreps):
    own_tile = amplitudes[:, 0]
    devices = lax.axis_size("pair")
    tiles_side = math.isqrt(devices)
    bit_count = tiles_side.bit_length() - 1
    position = lax.axis_index("pair")
    spread = lax.all_to_all(own_tile[None], "pair", split_axis=2, concat_axis=0, tiled=True)
    shape_rest = spread.shape[1:]
    spread = spread.reshape((tiles_side, tiles_side) + shape_rest)
    spread = jnp.swapaxes(spread, 0, 1).reshape((devices,) + shape_rest)
    mirrored = lax.all_to_all(spread, "pair", split_axis=0, concat_axis=2, tiled=True)[0]
    cycle_tile = (2.0 * own_tile.astype(F32) - mirrored.astype(F32)).astype(BF)
    cycle_stack = cycle_tile[None]
    for level in range(bit_count):
        partner = swapped(cycle_stack, "pair", level)
        lower_half = bit_of(position, level) == 0
        cycle_stack = jnp.where(
            lower_half,
            jnp.concatenate([cycle_stack, partner], axis=0),
            jnp.concatenate([partner, cycle_stack], axis=0),
        )
    weight_stack = w_ovvo
    for level in range(bit_count):
        partner = swapped(weight_stack, "pair", level + bit_count)
        lower_half = bit_of(position, level + bit_count) == 0
        weight_stack = jnp.where(
            lower_half,
            jnp.concatenate([weight_stack, partner], axis=0),
            jnp.concatenate([partner, weight_stack], axis=0),
        )
    partial_value = jnp.einsum(
        "kxac,kcb->xab", cycle_stack, weight_stack, preferred_element_type=F32
    )
    summed = lax.psum_scatter(
        partial_value.astype(BF), "virt", scatter_dimension=2, tiled=True
    ).astype(F32)
    width_local = summed.shape[2]
    occ_order = jnp.arange(occ_irreps.shape[0], dtype=jnp.int32)
    left_irrep = jnp.sum(jnp.where(occ_order == position // tiles_side, occ_irreps, 0))
    right_irrep = jnp.sum(jnp.where(occ_order == position % tiles_side, occ_irreps, 0))
    column_irreps = lax.dynamic_slice_in_dim(
        vir_irreps, lax.axis_index("virt") * width_local, width_local
    )
    target = jnp.bitwise_xor(left_irrep, right_irrep)
    allowed = jnp.bitwise_xor(vir_irreps[:, None], column_irreps[None, :]) == target
    return jnp.where(allowed[None], summed, 0.0).astype(BF)


def packed_kernel(
    starts_ref, colb_ref, amp_ref, w_ref, out_ref,
    T, S, W, R, cyc, C, Pk, U, D, Fin,
    t_send, t_recv, t_loc, a_send, a_recv, a_loc, f_send, s_send, s_recv,
    w2_send, w2_recv, w3_send, w3_recv, w3f_send, w3f_recv, y_send, y_recv,
    u_send, u_recv, d_send, d_recv,
):
    pair, v = lax.axis_index("pair"), lax.axis_index("virt")
    x, z = pair // NZ, pair % NZ
    half, l = z // O, z % O
    y, core = v // 2, v % 2

    def remote(src, dst, send, recv, p, q):
        return pltpu.make_async_remote_copy(
            src_ref=src, dst_ref=dst, send_sem=send, recv_sem=recv,
            device_id=(p, q), device_id_type=MESH,
        )

    def at(px, pz):
        return px * NZ + pz

    bar = pltpu.get_barrier_semaphore()

    def greet(p, q):
        pl.semaphore_signal(bar, inc=1, device_id=(p, q), device_id_type=MESH)

    for d in range(1, NV):
        greet(pair, (v + d) % NV)
    for d in range(1, NX):
        greet(at((x + d) % NX, z), v)
    for j in range(O):
        source = O * (l % 2) + j

        @pl.when(source != z)
        def _():
            greet(at(x, source), v)

    @pl.when(l > 0)
    def _():
        greet(at(x, z - 1), v)

    @pl.when(l < O - 1)
    def _():
        greet(at(x, z + 1), v)

    own_k = (l % 2 == half).astype(jnp.int32)
    ends = (l > 0).astype(jnp.int32) + (l < O - 1).astype(jnp.int32)
    pl.semaphore_wait(bar, (NV - 1) + (NX - 1) + O - own_k + ends)

    my_rows = pl.ds(pl.multiple_of(v * BV, BV), BV)

    def w_piece(q):
        return w_ref.at[0, :, pl.ds(pl.multiple_of(q * BV, BV), BV)]

    def t_copy(d):
        q = (v + d) % NV
        return remote(w_piece(q), T.at[my_rows], t_send.at[d - 1], t_recv.at[d - 1], pair, q)

    for d in range(1, NV):
        t_copy(d).start()
    t_local = pltpu.make_async_copy(w_piece(v), T.at[my_rows], t_loc)
    t_local.start()
    t_local.wait()
    for d in range(1, NV):
        t_copy(d).wait_recv()

    XR = V // NX

    def quarter(q):
        return pl.ds(pl.multiple_of(q * XR, XR), XR)

    def s_copy(d):
        q = (x + d) % NX
        return remote(T.at[quarter(q)], S.at[x], s_send.at[d - 1], s_recv.at[d - 1], at(q, z), v)

    for d in range(1, NX):
        s_copy(d).start()

    a_local = pltpu.make_async_copy(amp_ref.at[core, 0], R.at[v], a_loc)
    a_local.start()

    def a_sibling():
        return remote(amp_ref.at[1 - core, 0], R.at[v], a_send.at[4], a_recv.at[v], pair, v + 1 - 2 * core)

    def a_copy(dy, cc):
        return remote(
            amp_ref.at[cc, 0], R.at[v], a_send.at[(dy // 2) * 2 + cc], a_recv.at[v],
            pair, ((y + dy) % NY) * 2 + cc,
        )

    def a_arrived(g):
        remote(R.at[g], R.at[g], a_send.at[0], a_recv.at[g], pair, v + 1 - 2 * core).wait_recv()

    a_sibling().start()
    for cc in range(2):
        for dy in (1, 3):
            a_copy(dy, cc).start()

    def w2_copy(d, h):
        q = (x - d + NX) % NX
        src = T.at[quarter(x)] if d == 0 else S.at[q]
        dz = 2 * q + half + O * h
        return src, dz, remote(
            src, W.at[l, quarter(x)], w2_send.at[2 * d + h], w2_recv.at[l], at(x, dz), v
        )

    for d in range(NX):
        if d:
            s_copy(d).wait_recv()
        for h in range(2):
            src, dz, copy = w2_copy(d, h)

            @pl.when(dz != z)
            def _():
                copy.start()

            @pl.when(dz == z)
            def _():
                pltpu.make_async_copy(src, W.at[l, quarter(x)], w2_recv.at[l]).start()

    g_lo = ((y + 3) % NY) * 2
    g_hi = ((y + 1) % NY) * 2 + 1

    def f_copy(i):
        g, dy = ((g_lo, 1), (g_hi, 3))[i]
        return remote(R.at[g], R.at[g], f_send.at[i], a_recv.at[g], pair, ((y + dy) % NY) * 2 + core)

    a_arrived(g_lo)
    f_copy(0).start()
    a_arrived(g_hi)
    f_copy(1).start()

    def cycle_part(part, blocks):
        def body(i, carry):
            r = part * blocks + i
            row = pl.ds(pl.multiple_of(r * BV, BV), BV)
            for q in range(NV):
                mine = R[q, row, :].astype(F32)
                other = R[r, q * BV:(q + 1) * BV, :].astype(F32)
                cyc[core, row, q * BV:(q + 1) * BV] = (2.0 * mine - other.T).astype(BF)
            return carry

        lax.fori_loop(0, blocks, body, 0)

    def y_copy(part):
        rows = pl.ds(part * 256, 256)
        return remote(
            cyc.at[core, rows], cyc.at[core, rows], y_send.at[part], y_recv.at[part], pair, v + 1 - 2 * core
        )

    near = half == l % 2

    def order(n):
        offset = (0, 1, -1, 2, -2, 3, -3, 4)
        step = jnp.where(near, offset[n], offset[O - 1 - n])
        return (l + step + O) % O

    def w3_copy(n, way):
        j = order(n)
        block = W.at[j, quarter(x)]
        q = (x + (1, 3)[way]) % NX
        return remote(block, block, w3_send.at[way, n], w3_recv.at[way, j], at(q, z), v)

    def w3_arrived(n, way):
        j = order(n)
        block = W.at[j, quarter((x + (3, 1)[way]) % NX)]
        remote(block, block, w3_send.at[way, n], w3_recv.at[way, j], pair, v + 1 - 2 * core).wait_recv()

    def w3_forward(n):
        way = n % 2
        j = order(n)
        block = W.at[j, quarter((x + (3, 1)[way]) % NX)]
        q = (x + (1, 3)[way]) % NX
        return remote(block, block, w3f_send.at[n], w3f_recv.at[j], at(q, z), v)

    for n in range(O + 1):
        if n < O:
            j = order(n)
            block = W.at[j, quarter(x)]
            pltpu.make_async_copy(block, block, w2_recv.at[j]).wait()
            for way in range(2):
                w3_copy(n, way).start()
        if n > 0:
            w3_arrived(n - 1, (n - 1) % 2)
            w3_forward(n - 1).start()
        if n == 3:
            a_local.wait()
            a_arrived(v + 1 - 2 * core)
            a_arrived(g_lo + 1)
            a_arrived(g_hi - 1)
            a_arrived(((y + 2) % NY) * 2)
            a_arrived(((y + 2) % NY) * 2 + 1)
        if 3 <= n < 7:
            cycle_part(n - 3, 2)
            y_copy(n - 3).start()
    for n in range(O):
        w3_arrived(n, 1 - n % 2)
    for n in range(O):
        j = order(n)
        block = W.at[j, quarter((x + 2) % NX)]
        pltpu.make_async_copy(block, block, w3f_recv.at[j]).wait()
    for part in range(4):
        rows = pl.ds(part * 256, 256)
        block = cyc.at[1 - core, rows]
        pltpu.make_async_copy(block, block, y_recv.at[part]).wait()

    colb = jnp.broadcast_to(colb_ref[0:1, :], (CAP, BV))

    def products(s):
        weights = jnp.concatenate([W[O - 1 - s], W[s]], axis=1)

        def body(i, carry):
            xx, m = i // 4, i % 4
            rows = pl.ds(pl.multiple_of(m * 256, 256), 256)
            value = jnp.dot(cyc[xx, rows, :], weights, preferred_element_type=F32)
            C[pl.ds(pl.multiple_of(i * 256, 256), 256), :] = value[:, :BV]
            C[pl.ds(pl.multiple_of(i * 256 + 2 * V, 256), 256), :] = value[:, BV:]
            return carry

        lax.fori_loop(0, 8, body, 0)

        for side in range(2):
            j = (O - 1 - s, s)[side]
            for xx in range(2):
                acc = jnp.zeros((CAP, BV), F32)
                for beta in range(O):
                    start = starts_ref[j, beta] * 8 + (side * 2 + xx) * V
                    acc = jnp.where(colb == beta, C[pl.ds(start, CAP), :], acc)
                Pk[j, xx] = acc.astype(BF)

    def hop(buf, send, recv, j, xx, step):
        return remote(buf.at[j, xx], buf.at[j, xx], send.at[j, xx], recv.at[j, xx], at(x, z + step), v)

    def flow(buf, send, recv, j, xx, step, first):
        @pl.when(first)
        def _():
            buf[j, xx] = Pk[j, xx]

        @pl.when(jnp.logical_not(first))
        def _():
            hop(buf, send, recv, j, xx, step).wait_recv()
            buf[j, xx] = (buf[j, xx].astype(F32) + Pk[j, xx].astype(F32)).astype(BF)

        hop(buf, send, recv, j, xx, step).start()

    def tick(tau, carry):
        @pl.when(tau < 4)
        def _():
            products(tau)

        for xx in range(2):
            @pl.when(tau >= l)
            def _():
                flow(U, u_send, u_recv, O - 1 + l - tau, xx, 1, l == 0)

            @pl.when(tau >= O - 1 - l)
            def _():
                flow(D, d_send, d_recv, l - (O - 1 - tau), xx, -1, l == O - 1)

        return carry

    lax.fori_loop(0, O - 1, tick, 0)

    Fin[...] = Pk[l].astype(F32)
    for xx in range(2):
        @pl.when(l > 0)
        def _():
            hop(U, u_send, u_recv, l, xx, 1).wait_recv()
            Fin[xx] += U[l, xx].astype(F32)

        @pl.when(l < O - 1)
        def _():
            hop(D, d_send, d_recv, l, xx, -1).wait_recv()
            Fin[xx] += D[l, xx].astype(F32)

    out_ref[...] = Fin[...].astype(BF)

    for d in range(1, NV):
        t_copy(d).wait_send()
    for d in range(1, NX):
        s_copy(d).wait_send()
    a_sibling().wait_send()
    for cc in range(2):
        for dy in (1, 3):
            a_copy(dy, cc).wait_send()
    for d in range(NX):
        for h in range(2):
            _, dz, copy = w2_copy(d, h)

            @pl.when(dz != z)
            def _():
                copy.wait_send()
    for i in range(2):
        f_copy(i).wait_send()
    for n in range(O):
        w3_copy(n, 0).wait_send()
        w3_copy(n, 1).wait_send()
        w3_forward(n).wait_send()
    for part in range(4):
        y_copy(part).wait_send()

    def drain(j, carry):
        for xx in range(2):
            @pl.when(j > l)
            def _():
                hop(U, u_send, u_recv, j, xx, 1).wait_send()

            @pl.when(j < l)
            def _():
                hop(D, d_send, d_recv, j, xx, -1).wait_send()

        return carry

    lax.fori_loop(0, O, drain, 0)


def unpack_kernel(start_ref, begin_ref, end_ref, target_ref, colb_ref, packed_ref, out_ref, wide):
    target = target_ref[0]
    STEP = 32
    wide[:, STEP:STEP + CAP, :] = packed_ref[...].astype(F32)
    colb = jnp.broadcast_to(colb_ref[0:1, :], (STEP, BV))
    row = lax.broadcasted_iota(jnp.int32, (STEP, BV), 0)

    def body(i, carry):
        first = pl.multiple_of(i * STEP, STEP)
        acc = [jnp.zeros((STEP, BV), F32)] * 2
        for alpha in range(O):
            at = jnp.clip(first - start_ref[alpha], -STEP, CAP) + STEP
            at = pl.multiple_of(at, 8)
            inside = (row + first >= begin_ref[alpha]) & (row + first < end_ref[alpha])
            inside = inside & (colb == jnp.bitwise_xor(target, alpha))
            for xx in range(2):
                acc[xx] = jnp.where(inside, wide[xx, pl.ds(at, STEP), :], acc[xx])
        for xx in range(2):
            out_ref[xx, pl.ds(first, STEP), :] = acc[xx].astype(BF)
        return carry

    lax.fori_loop(0, V // STEP, body, 0)


def packed(tables, amplitudes, w_ovvo):
    starts, start, begin, end, target, colb = tables
    smem = pl.BlockSpec(memory_space=pltpu.SMEM)
    vmem = pl.BlockSpec(memory_space=pltpu.VMEM)
    anym = pl.BlockSpec(memory_space=pl.ANY)
    dma = pltpu.SemaphoreType.DMA
    small = pl.pallas_call(
        packed_kernel,
        out_shape=jax.ShapeDtypeStruct((2, CAP, BV), BF),
        in_specs=[smem, vmem, anym, anym],
        out_specs=vmem,
        scratch_shapes=[
            pltpu.VMEM((V, BV), BF),
            pltpu.VMEM((NX, V // NX, BV), BF),
            pltpu.VMEM((O, V, BV), BF),
            pltpu.VMEM((NV, V, BV), BF),
            pltpu.VMEM((2, V, V), BF),
            pltpu.VMEM((4 * V, BV), F32),
            pltpu.VMEM((O, 2, CAP, BV), BF),
            pltpu.VMEM((O, 2, CAP, BV), BF),
            pltpu.VMEM((O, 2, CAP, BV), BF),
            pltpu.VMEM((2, CAP, BV), F32),
            dma((7,)), dma((7,)), dma, dma((5,)), dma((NV,)), dma, dma((2,)), dma((3,)), dma((3,)),
            dma((8,)), dma((O,)), dma((2, O)), dma((2, O)), dma((O,)), dma((O,)), dma((4,)), dma((4,)),
            dma((O, 2)), dma((O, 2)), dma((O, 2)), dma((O, 2)),
        ],
        compiler_params=pltpu.CompilerParams(
            collective_id=0, has_side_effects=True, vmem_limit_bytes=40 * 2**20
        ),
        name="packed_cycle",
    )(starts, colb, amplitudes, w_ovvo)
    return pl.pallas_call(
        unpack_kernel,
        out_shape=jax.ShapeDtypeStruct((2, V, BV), BF),
        in_specs=[smem, smem, smem, smem, vmem, vmem],
        out_specs=vmem,
        scratch_shapes=[pltpu.VMEM((2, CAP + 64, BV), F32)],
        name="unpack",
    )(start, begin, end, target, colb, small)


def shards(amplitudes, w_ovvo, occ_irreps, vir_irreps):
    position = lax.axis_index("pair")
    left, right = position // O, position % O
    irreps = jnp.arange(O, dtype=jnp.int32)
    below = vir_irreps[None, :] < irreps[:, None]
    upto = vir_irreps[None, :] <= irreps[:, None]
    begin = jnp.sum(below.astype(jnp.int32), axis=1)
    end = jnp.sum(upto.astype(jnp.int32), axis=1)
    start = jnp.minimum(begin // 8 * 8, V - CAP)
    fits = jnp.all(end - start <= CAP)
    occ_left = jnp.sum(jnp.where(irreps == left, occ_irreps, 0))
    occ_right = jnp.sum(jnp.where(irreps == right, occ_irreps, 0))
    target = jnp.bitwise_xor(occ_left, occ_right)[None]
    alpha = jnp.bitwise_xor(jnp.bitwise_xor(occ_left, occ_irreps)[:, None], irreps[None, :])
    starts = jnp.sum(jnp.where(alpha[:, :, None] == irreps, start // 8, 0), axis=2)
    colb = lax.dynamic_slice_in_dim(vir_irreps, lax.axis_index("virt") * BV, BV)
    colb = jnp.broadcast_to(colb[None, :], (8, BV))
    tables = (starts, start, begin, end, target, colb)
    result = lax.cond(
        fits,
        lambda: packed(tables, amplitudes, w_ovvo),
        lambda: general(amplitudes, w_ovvo, occ_irreps, vir_irreps),
    )
    return result[:, None]


def solution(mesh):
    in_specs = (P(None, "pair", None, "virt"), P("pair", "virt", None), P(), P())
    out_specs = P(None, "pair", None, "virt")
    return jax.shard_map(shards, mesh=mesh, in_specs=in_specs, out_specs=out_specs, check_vma=False)
```

```python
import functools
import math

import jax
import jax.numpy as jnp
from jax import lax
from jax.experimental import pallas as pl
from jax.experimental.pallas import tpu as pltpu
from jax.sharding import PartitionSpec as P

MESH = pl.DeviceIdType.MESH
BF = jnp.bfloat16
F32 = jnp.float32

NX, NZ, NY = 4, 16, 4
O = 8
NV = 8
V = 1024
BV = 128
CAP = 288


def swapped(block, axis, stride):
    count = lax.axis_size(axis)
    route = []
    for low in range(count):
        high = low | 1 << stride
        if high != low and high < count:
            route += [(low, high), (high, low)]
    return lax.ppermute(block, axis, route)


def bit_of(position, level):
    return position // 2**level % 2


def general(amplitudes, w_ovvo, occ_irreps, vir_irreps):
    own_tile = amplitudes[:, 0]
    devices = lax.axis_size("pair")
    tiles_side = math.isqrt(devices)
    bit_count = tiles_side.bit_length() - 1
    position = lax.axis_index("pair")
    spread = lax.all_to_all(own_tile[None], "pair", split_axis=2, concat_axis=0, tiled=True)
    shape_rest = spread.shape[1:]
    spread = spread.reshape((tiles_side, tiles_side) + shape_rest)
    spread = jnp.swapaxes(spread, 0, 1).reshape((devices,) + shape_rest)
    mirrored = lax.all_to_all(spread, "pair", split_axis=0, concat_axis=2, tiled=True)[0]
    cycle_tile = (2.0 * own_tile.astype(F32) - mirrored.astype(F32)).astype(BF)
    cycle_stack = cycle_tile[None]
    for level in range(bit_count):
        partner = swapped(cycle_stack, "pair", level)
        lower_half = bit_of(position, level) == 0
        cycle_stack = jnp.where(
            lower_half,
            jnp.concatenate([cycle_stack, partner], axis=0),
            jnp.concatenate([partner, cycle_stack], axis=0),
        )
    weight_stack = w_ovvo
    for level in range(bit_count):
        partner = swapped(weight_stack, "pair", level + bit_count)
        lower_half = bit_of(position, level + bit_count) == 0
        weight_stack = jnp.where(
            lower_half,
            jnp.concatenate([weight_stack, partner], axis=0),
            jnp.concatenate([partner, weight_stack], axis=0),
        )
    partial_value = jnp.einsum(
        "kxac,kcb->xab", cycle_stack, weight_stack, preferred_element_type=F32
    )
    pieces = lax.all_to_all(
        partial_value.astype(BF)[None], "virt", split_axis=3, concat_axis=0, tiled=True
    )
    summed = jnp.sum(pieces.astype(F32), axis=0)
    width_local = summed.shape[2]
    occ_order = jnp.arange(occ_irreps.shape[0], dtype=jnp.int32)
    left_irrep = jnp.sum(jnp.where(occ_order == position // tiles_side, occ_irreps, 0))
    right_irrep = jnp.sum(jnp.where(occ_order == position % tiles_side, occ_irreps, 0))
    column_irreps = lax.dynamic_slice_in_dim(
        vir_irreps, lax.axis_index("virt") * width_local, width_local
    )
    target = jnp.bitwise_xor(left_irrep, right_irrep)
    allowed = jnp.bitwise_xor(vir_irreps[:, None], column_irreps[None, :]) == target
    return jnp.where(allowed[None], summed, 0.0).astype(BF)


PAD = 32
FR = CAP + 2 * PAD
NG = 4
GW = V // NG


def packed_kernel(
    occ_ref, vir_ref, amp_ref, w_ref, out_ref, fits_ref,
    T, S, W, R, cyc, C, Pk, U, D, Fin, key, st,
    t_send, t_recv, a_send, a_recv, f_send, s_send, s_recv,
    w2_send, w2_recv, w3_send, w3_recv, w3f_send, w3f_recv, y_send, y_recv,
    u_send, u_recv, d_send, d_recv,
):
    pair, v = lax.axis_index("pair"), lax.axis_index("virt")
    x, z = pair // NZ, pair % NZ
    half, l = z // O, z % O
    y, core = v // 2, v % 2
    sibling = v + 1 - 2 * core

    def remote(src, dst, send, recv, p, q):
        return pltpu.make_async_remote_copy(
            src_ref=src, dst_ref=dst, send_sem=send, recv_sem=recv,
            device_id=(p, q), device_id_type=MESH,
        )

    def arrived(block, sem):
        pltpu.make_async_copy(block, block, sem).wait()

    def at(px, pz):
        return px * NZ + pz

    bar = pltpu.get_barrier_semaphore()

    def greet(p, q):
        pl.semaphore_signal(bar, inc=1, device_id=(p, q), device_id_type=MESH)

    for d in range(1, NV):
        greet(pair, (v + d) % NV)
    for d in range(1, NX):
        greet(at((x + d) % NX, z), v)
    for j in range(O):
        source = O * (l % 2) + j

        @pl.when(source != z)
        def _():
            greet(at(x, source), v)

    @pl.when(l > 0)
    def _():
        greet(at(x, z - 1), v)

    @pl.when(l < O - 1)
    def _():
        greet(at(x, z + 1), v)

    own_k = (l % 2 == half).astype(jnp.int32)
    ends = (l > 0).astype(jnp.int32) + (l < O - 1).astype(jnp.int32)
    pl.semaphore_wait(bar, (NV - 1) + (NX - 1) + O - own_k + ends)

    def w_piece(q):
        return w_ref.at[0, :, pl.ds(pl.multiple_of(q * BV, BV), BV)]

    def t_copy(d):
        q = (v + d) % NV
        return remote(w_piece(q), T.at[v], t_send.at[d - 1], t_recv.at[v], pair, q)

    t_local = pltpu.make_async_copy(w_piece(v), T.at[v], t_recv.at[v])
    t_local.start()
    for d in range(1, NV):
        t_copy(d).start()

    a_local = pltpu.make_async_copy(amp_ref.at[core, 0], R.at[v], a_recv.at[v])
    a_local.start()

    def a_sibling():
        return remote(amp_ref.at[1 - core, 0], R.at[v], a_send.at[4], a_recv.at[v], pair, sibling)

    def a_copy(dy, cc):
        return remote(
            amp_ref.at[cc, 0], R.at[v], a_send.at[(dy // 2) * 2 + cc], a_recv.at[v],
            pair, ((y + dy) % NY) * 2 + cc,
        )

    def a_arrived(g):
        arrived(R.at[g], a_recv.at[g])

    a_sibling().start()
    for cc in range(2):
        for dy in (1, 3):
            a_copy(dy, cc).start()

    XR = BV // NX

    def chunk(n):
        return (y + n) % NY

    def blocks(n):
        return pl.ds(2 * chunk(n), 2)

    def quarter(q):
        return pl.ds(pl.multiple_of(q * XR, XR), XR)

    def s_copy(n, d):
        q = (x + d) % NX
        return remote(
            T.at[blocks(n), quarter(q)], S.at[x, blocks(n)],
            s_send.at[n, d - 1], s_recv.at[n, d - 1], at(q, z), v,
        )

    def spread_x(n):
        for i in range(2):
            g = 2 * chunk(n) + i
            arrived(T.at[g], t_recv.at[g])
        for d in range(1, NX):
            s_copy(n, d).start()

    def w2_copy(n, d, h):
        q = (x - d + NX) % NX
        src = T.at[blocks(n), quarter(x)] if d == 0 else S.at[q, blocks(n)]
        dst = W.at[l, blocks(n), quarter(x)]
        dz = 2 * q + half + O * h
        return dz, src, dst, remote(src, dst, w2_send.at[n, 2 * d + h], w2_recv.at[n, l], at(x, dz), v)

    def move_z(n):
        for d in range(NX):
            if d:
                q = (x - d + NX) % NX
                arrived(S.at[q, blocks(n)], s_recv.at[n, d - 1])
            for h in range(2):
                dz, src, dst, copy = w2_copy(n, d, h)

                @pl.when(dz != z)
                def _():
                    copy.start()

                @pl.when(dz == z)
                def _():
                    pltpu.make_async_copy(src, dst, w2_recv.at[n, l]).start()

    def left_z(n):
        for d in range(NX):
            for h in range(2):
                dz, _, _, copy = w2_copy(n, d, h)

                @pl.when(dz != z)
                def _():
                    copy.wait_send()

    def w3_copy(n, way):
        block = W.at[:, blocks(n), quarter(x)]
        return remote(block, block, w3_send.at[n, way], w3_recv.at[n, way], at((x + (1, 3)[way]) % NX, z), v)

    def gather_x(n):
        for j in range(O):
            arrived(W.at[j, blocks(n), quarter(x)], w2_recv.at[n, j])
        for way in range(2):
            w3_copy(n, way).start()

    def w3_forward(n, way):
        block = W.at[pl.ds(4 * way, 4), blocks(n), quarter((x + (3, 1)[way]) % NX)]
        return remote(block, block, w3f_send.at[n, way], w3f_recv.at[n, way], at((x + (1, 3)[way]) % NX, z), v)

    def forward_x(n):
        for way in range(2):
            arrived(W.at[:, blocks(n), quarter((x + (3, 1)[way]) % NX)], w3_recv.at[n, way])
            w3_forward(n, way).start()

    def gathered_x(n):
        for way in range(2):
            arrived(W.at[pl.ds(4 * way, 4), blocks(n), quarter((x + 2) % NX)], w3f_recv.at[n, way])

    g_lo = ((y + 3) % NY) * 2
    g_hi = ((y + 1) % NY) * 2 + 1

    def f_copy(i):
        g, dy = ((g_lo, 1), (g_hi, 3))[i]
        return remote(R.at[g], R.at[g], f_send.at[i], a_recv.at[g], pair, ((y + dy) % NY) * 2 + core)

    def cycle_part(part):
        def body(i, carry):
            r = part * 2 + i
            row = pl.ds(pl.multiple_of(r * BV, BV), BV)
            for q in range(NV):
                mine = R[q, row, :].astype(F32)
                other = R[r, q * BV:(q + 1) * BV, :].astype(F32)
                cyc[core, row, q * BV:(q + 1) * BV] = (2.0 * mine - other.T).astype(BF)
            return carry

        lax.fori_loop(0, 2, body, 0)
        y_copy(part).start()

    def y_copy(part):
        rows = pl.ds(part * 256, 256)
        return remote(
            cyc.at[core, rows], cyc.at[core, rows], y_send.at[part], y_recv.at[part], pair, sibling
        )

    irreps = vir_ref[...]
    begin = [jnp.sum((irreps < alpha).astype(jnp.int32)) for alpha in range(1, O)]
    begin = [jnp.int32(0)] + begin + [jnp.int32(V)]

    def tables():
        good = jnp.int32(1)
        for alpha in range(O):
            first = jnp.minimum(lax.shift_right_logical(begin[alpha], 3), (V - CAP) // 8)
            st[alpha] = first
            good = jnp.where(begin[alpha + 1] - first * 8 <= CAP, good, 0)
        fits_ref[0] = good
        target = jnp.bitwise_xor(occ_ref[pair // O], occ_ref[pair % O])
        columns = jnp.bitwise_xor(jnp.broadcast_to(vir_ref[pl.ds(v, 1), :], (BV, BV)), target)
        row = lax.broadcasted_iota(jnp.int32, (BV, BV), 0)

        def body(i, carry):
            own = jnp.zeros((BV, BV), jnp.int32)
            for alpha in range(1, O):
                own = own + (row + i * BV >= begin[alpha]).astype(jnp.int32)
            key[pl.ds(pl.multiple_of(i * BV, BV), BV), :] = jnp.where(own == columns, own, -1)
            return carry

        lax.fori_loop(0, V // BV, body, 0)

    def product(n, s):
        g = chunk(n)
        weights = jnp.concatenate(
            [W[O - 1 - s, blocks(n)].reshape(GW, BV), W[s, blocks(n)].reshape(GW, BV)], axis=1
        )
        columns = pl.ds(pl.multiple_of(g * GW, GW), GW)

        def body(xx, carry):
            for m in range(4):
                value = jnp.dot(
                    cyc[xx, pl.ds(m * 256, 256), columns], weights, preferred_element_type=F32
                )
                for side in range(2):
                    j = (O - 1 - s, s)[side]
                    rows = pl.ds(pl.multiple_of((j * 2 + xx) * V + m * 256, 256), 256)
                    part = value[:, side * BV:(side + 1) * BV]
                    C[rows, :] = part if n == 0 else C[rows, :] + part
            return carry

        lax.fori_loop(0, 2, body, 0)

    def products(n):
        def body(s, carry):
            product(n, s)
            return carry

        lax.fori_loop(0, 4, body, 0)

    for n in range(NG):
        spread_x(n)
    move_z(0)
    move_z(1)
    tables()
    a_arrived(g_lo)
    f_copy(0).start()
    a_arrived(g_hi)
    f_copy(1).start()
    left_z(0)
    move_z(2)
    gather_x(0)
    forward_x(0)
    left_z(1)
    move_z(3)
    gather_x(1)
    a_arrived(v)
    a_arrived(sibling)
    a_arrived(g_lo + 1)
    a_arrived(g_hi - 1)
    a_arrived(((y + 2) % NY) * 2)
    a_arrived(((y + 2) % NY) * 2 + 1)
    cycle_part(0)
    cycle_part(1)
    forward_x(1)
    gather_x(2)
    cycle_part(2)
    cycle_part(3)
    forward_x(2)
    gathered_x(0)
    for part in range(4):
        arrived(cyc.at[1 - core, pl.ds(part * 256, 256)], y_recv.at[part])
    products(0)
    gather_x(3)
    gathered_x(1)
    products(1)
    forward_x(3)
    gathered_x(2)
    products(2)
    gathered_x(3)

    colb = jnp.broadcast_to(vir_ref[pl.ds(v, 1), :], (CAP, BV))
    occ_left = occ_ref[pair // O]

    def pack(s):
        for side in range(2):
            j = (O - 1 - s, s)[side]
            target = jnp.bitwise_xor(occ_left, occ_ref[j])
            for xx in range(2):
                acc = jnp.zeros((CAP, BV), F32)
                for beta in range(O):
                    start = st[jnp.bitwise_xor(target, beta)] * 8 + (j * 2 + xx) * V
                    acc = jnp.where(colb == beta, C[pl.ds(start, CAP), :], acc)
                Pk[j, xx] = acc.astype(BF)

    def hop(buf, send, recv, j, xx, step):
        return remote(buf.at[j, xx], buf.at[j, xx], send.at[j, xx], recv.at[j, xx], at(x, z + step), v)

    def flow(buf, send, recv, j, xx, step, first):
        @pl.when(first)
        def _():
            buf[j, xx] = Pk[j, xx]

        @pl.when(jnp.logical_not(first))
        def _():
            hop(buf, send, recv, j, xx, step).wait_recv()
            buf[j, xx] = (buf[j, xx].astype(F32) + Pk[j, xx].astype(F32)).astype(BF)

        hop(buf, send, recv, j, xx, step).start()

    def tick(tau, carry):
        @pl.when(tau < 4)
        def _():
            product(NG - 1, tau)
            pack(tau)

        for xx in range(2):
            @pl.when(tau >= l)
            def _():
                flow(U, u_send, u_recv, O - 1 + l - tau, xx, 1, l == 0)

            @pl.when(tau >= O - 1 - l)
            def _():
                flow(D, d_send, d_recv, l - (O - 1 - tau), xx, -1, l == O - 1)

        return carry

    lax.fori_loop(0, O - 1, tick, 0)

    for xx in range(2):
        mid = pl.ds(xx * FR + PAD, CAP)
        Fin[mid, :] = Pk[l, xx].astype(F32)

        @pl.when(l > 0)
        def _():
            hop(U, u_send, u_recv, l, xx, 1).wait_recv()
            Fin[mid, :] += U[l, xx].astype(F32)

        @pl.when(l < O - 1)
        def _():
            hop(D, d_send, d_recv, l, xx, -1).wait_recv()
            Fin[mid, :] += D[l, xx].astype(F32)

        def unpack(i, carry):
            rows = pl.ds(pl.multiple_of(i * PAD, PAD), PAD)
            held = key[rows, :]
            acc = jnp.zeros((PAD, BV), F32)
            for alpha in range(O):
                first = jnp.clip(i * (PAD // 8) - st[alpha], -PAD // 8, CAP // 8) + PAD // 8
                acc = jnp.where(held == alpha, Fin[pl.ds(first * 8 + xx * FR, PAD), :], acc)
            out_ref[xx, rows, :] = acc.astype(BF)
            return carry

        lax.fori_loop(0, V // PAD, unpack, 0)

    for d in range(1, NV):
        t_copy(d).wait_send()
    a_sibling().wait_send()
    for cc in range(2):
        for dy in (1, 3):
            a_copy(dy, cc).wait_send()
    for i in range(2):
        f_copy(i).wait_send()
    for n in range(NG):
        for d in range(1, NX):
            s_copy(n, d).wait_send()
        if n >= 2:
            left_z(n)
        for way in range(2):
            w3_copy(n, way).wait_send()
            w3_forward(n, way).wait_send()
    for part in range(4):
        y_copy(part).wait_send()

    def drain(j, carry):
        for xx in range(2):
            @pl.when(j > l)
            def _():
                hop(U, u_send, u_recv, j, xx, 1).wait_send()

            @pl.when(j < l)
            def _():
                hop(D, d_send, d_recv, j, xx, -1).wait_send()

        return carry

    lax.fori_loop(0, O, drain, 0)


def packed(amplitudes, w_ovvo, occ_irreps, vir_irreps):
    smem = pl.BlockSpec(memory_space=pltpu.SMEM)
    vmem = pl.BlockSpec(memory_space=pltpu.VMEM)
    anym = pl.BlockSpec(memory_space=pl.ANY)
    dma = pltpu.SemaphoreType.DMA
    return pl.pallas_call(
        packed_kernel,
        out_shape=(jax.ShapeDtypeStruct((2, V, BV), BF), jax.ShapeDtypeStruct((1,), jnp.int32)),
        in_specs=[smem, vmem, anym, anym],
        out_specs=(vmem, smem),
        scratch_shapes=[
            pltpu.VMEM((NV, BV, BV), BF),
            pltpu.VMEM((NX, NV, BV // NX, BV), BF),
            pltpu.VMEM((O, NV, BV, BV), BF),
            pltpu.VMEM((NV, V, BV), BF),
            pltpu.VMEM((2, V, V), BF),
            pltpu.VMEM((O * 2 * V, BV), F32),
            pltpu.VMEM((O, 2, CAP, BV), BF),
            pltpu.VMEM((O, 2, CAP, BV), BF),
            pltpu.VMEM((O, 2, CAP, BV), BF),
            pltpu.VMEM((2 * FR, BV), F32),
            pltpu.VMEM((V, BV), jnp.int32),
            pltpu.SMEM((O,), jnp.int32),
            dma((7,)), dma((NV,)), dma((5,)), dma((NV,)), dma((2,)), dma((NG, 3)), dma((NG, 3)),
            dma((NG, 8)), dma((NG, O)), dma((NG, 2)), dma((NG, 2)), dma((NG, 2)), dma((NG, 2)), dma((4,)), dma((4,)),
            dma((O, 2)), dma((O, 2)), dma((O, 2)), dma((O, 2)),
        ],
        compiler_params=pltpu.CompilerParams(
            collective_id=0, has_side_effects=True, vmem_limit_bytes=48 * 2**20
        ),
        name="packed_cycle",
    )(occ_irreps, vir_irreps.reshape(V // BV, BV), amplitudes, w_ovvo)


def shards(amplitudes, w_ovvo, occ_irreps, vir_irreps):
    result, fits = packed(amplitudes, w_ovvo, occ_irreps, vir_irreps)
    result = lax.cond(
        fits[0] == 1,
        lambda: result,
        lambda: general(amplitudes, w_ovvo, occ_irreps, vir_irreps),
    )
    return result[:, None]


def solution(mesh):
    in_specs = (P(None, "pair", None, "virt"), P("pair", "virt", None), P(), P())
    out_specs = P(None, "pair", None, "virt")
    return jax.shard_map(shards, mesh=mesh, in_specs=in_specs, out_specs=out_specs, check_vma=False)
```

```python
import functools
import math

import jax
import jax.numpy as jnp
from jax import lax
from jax.experimental import pallas as pl
from jax.experimental.pallas import tpu as pltpu
from jax.sharding import PartitionSpec as P

MESH = pl.DeviceIdType.MESH
BF = jnp.bfloat16
F32 = jnp.float32

NX, NZ, NY = 4, 16, 4
O = 8
NV = 8
V = 1024
BV = 128
CAP = 288


def swapped(block, axis, stride):
    count = lax.axis_size(axis)
    route = []
    for low in range(count):
        high = low | 1 << stride
        if high != low and high < count:
            route += [(low, high), (high, low)]
    return lax.ppermute(block, axis, route)


def bit_of(position, level):
    return position // 2**level % 2


def general(amplitudes, w_ovvo, occ_irreps, vir_irreps):
    own_tile = amplitudes[:, 0]
    devices = lax.axis_size("pair")
    tiles_side = math.isqrt(devices)
    bit_count = tiles_side.bit_length() - 1
    position = lax.axis_index("pair")
    spread = lax.all_to_all(own_tile[None], "pair", split_axis=2, concat_axis=0, tiled=True)
    shape_rest = spread.shape[1:]
    spread = spread.reshape((tiles_side, tiles_side) + shape_rest)
    spread = jnp.swapaxes(spread, 0, 1).reshape((devices,) + shape_rest)
    mirrored = lax.all_to_all(spread, "pair", split_axis=0, concat_axis=2, tiled=True)[0]
    cycle_tile = (2.0 * own_tile.astype(F32) - mirrored.astype(F32)).astype(BF)
    cycle_stack = cycle_tile[None]
    for level in range(bit_count):
        partner = swapped(cycle_stack, "pair", level)
        lower_half = bit_of(position, level) == 0
        cycle_stack = jnp.where(
            lower_half,
            jnp.concatenate([cycle_stack, partner], axis=0),
            jnp.concatenate([partner, cycle_stack], axis=0),
        )
    weight_stack = w_ovvo
    for level in range(bit_count):
        partner = swapped(weight_stack, "pair", level + bit_count)
        lower_half = bit_of(position, level + bit_count) == 0
        weight_stack = jnp.where(
            lower_half,
            jnp.concatenate([weight_stack, partner], axis=0),
            jnp.concatenate([partner, weight_stack], axis=0),
        )
    partial_value = jnp.einsum(
        "kxac,kcb->xab", cycle_stack, weight_stack, preferred_element_type=F32
    )
    pieces = lax.all_to_all(
        partial_value.astype(BF)[None], "virt", split_axis=3, concat_axis=0, tiled=True
    )
    summed = jnp.sum(pieces.astype(F32), axis=0)
    width_local = summed.shape[2]
    occ_order = jnp.arange(occ_irreps.shape[0], dtype=jnp.int32)
    left_irrep = jnp.sum(jnp.where(occ_order == position // tiles_side, occ_irreps, 0))
    right_irrep = jnp.sum(jnp.where(occ_order == position % tiles_side, occ_irreps, 0))
    column_irreps = lax.dynamic_slice_in_dim(
        vir_irreps, lax.axis_index("virt") * width_local, width_local
    )
    target = jnp.bitwise_xor(left_irrep, right_irrep)
    allowed = jnp.bitwise_xor(vir_irreps[:, None], column_irreps[None, :]) == target
    return jnp.where(allowed[None], summed, 0.0).astype(BF)


PAD = 32
FR = CAP + 2 * PAD
NG = 4
NP = 2
PR = CAP // NP
GW = V // NG


def packed_kernel(
    occ_ref, vir_ref, amp_ref, w_ref, out_ref, fits_ref,
    S, W, R, cyc, C, Pk, U, D, Fin, key, st,
    a_send, a_recv, f_send, s_send, s_recv,
    w2_send, w2_recv, w3_send, w3_recv, w3f_send, w3f_recv, y_send, y_recv,
    u_send, u_recv, d_send, d_recv,
):
    pair, v = lax.axis_index("pair"), lax.axis_index("virt")
    x, z = pair // NZ, pair % NZ
    half, l = z // O, z % O
    y, core = v // 2, v % 2
    sibling = v + 1 - 2 * core

    def remote(src, dst, send, recv, p, q):
        return pltpu.make_async_remote_copy(
            src_ref=src, dst_ref=dst, send_sem=send, recv_sem=recv,
            device_id=(p, q), device_id_type=MESH,
        )

    def arrived(block, sem):
        pltpu.make_async_copy(block, block, sem).wait()

    def at(px, pz):
        return px * NZ + pz

    bar = pltpu.get_barrier_semaphore()

    def greet(p, q):
        pl.semaphore_signal(bar, inc=1, device_id=(p, q), device_id_type=MESH)

    for d in range(1, NX * NV):
        greet(at((x + d // NV) % NX, z), (v + d) % NV)
    for j in range(O):
        source = O * (l % 2) + j

        @pl.when(source != z)
        def _():
            greet(at(x, source), v)

    @pl.when(l > 0)
    def _():
        greet(at(x, z - 1), v)

    @pl.when(l < O - 1)
    def _():
        greet(at(x, z + 1), v)

    own_k = (l % 2 == half).astype(jnp.int32)
    ends = (l > 0).astype(jnp.int32) + (l < O - 1).astype(jnp.int32)
    pl.semaphore_wait(bar, NX * NV - 1 + O - own_k + ends)

    XR = BV // NX

    def chunk(n):
        return (y + n) % NY

    def blocks(n):
        return pl.ds(2 * chunk(n), 2)

    def quarter(q):
        return pl.ds(pl.multiple_of(q * XR, XR), XR)

    def s_copy(n, c, d):
        p, q = (x + d) % NX, ((y - n + NY) % NY) * 2 + (core + c) % 2
        src = w_ref.at[0, quarter(p), pl.ds(pl.multiple_of(q * BV, BV), BV)]
        if n + c + d == 0:
            return pltpu.make_async_copy(src, S.at[x, v], s_recv.at[x, v])
        return remote(src, S.at[x, v], s_send.at[n, c, d], s_recv.at[x, v], at(p, z), q)

    spread = [(n, c, d) for n in range(NG) for c in range(2) for d in range(NX)]
    for which in spread:
        s_copy(*which).start()

    a_local = pltpu.make_async_copy(amp_ref.at[core, 0], R.at[v], a_recv.at[v])
    a_local.start()

    def a_sibling():
        return remote(amp_ref.at[1 - core, 0], R.at[v], a_send.at[4], a_recv.at[v], pair, sibling)

    def a_copy(dy, cc):
        return remote(
            amp_ref.at[cc, 0], R.at[v], a_send.at[(dy // 2) * 2 + cc], a_recv.at[v],
            pair, ((y + dy) % NY) * 2 + cc,
        )

    def a_arrived(g):
        arrived(R.at[g], a_recv.at[g])

    odd = (half + l) % 2

    def w2_copy(n, slot, way):
        hops = 2 * slot + 2 - odd
        step = (hops, -hops)[way]
        q = ((l + step + O) % O) // 2
        src, dst = S.at[q, blocks(n)], W.at[l, blocks(n), quarter(x)]
        dz = (z + step + NZ) % NZ
        return src, dst, remote(src, dst, w2_send.at[n, slot, way], w2_recv.at[n, l], at(x, dz), v)

    def move_z(n):
        for q in range(NX):
            for c in range(2):
                g = 2 * chunk(n) + c
                arrived(S.at[q, g], s_recv.at[q, g])
        for slot in (3, 2, 1, 0):
            src, dst, up = w2_copy(n, slot, 0)
            up.start()
            src, dst, down = w2_copy(n, slot, 1)
            if slot < 3:
                down.start()
            else:
                @pl.when(odd == 1)
                def _():
                    down.start()

                @pl.when(odd == 0)
                def _():
                    pltpu.make_async_copy(src, dst, w2_recv.at[n, l]).start()

    def left_z(n):
        for slot in (3, 2, 1, 0):
            w2_copy(n, slot, 0)[2].wait_send()
            down = w2_copy(n, slot, 1)[2]
            if slot < 3:
                down.wait_send()
            else:
                @pl.when(odd == 1)
                def _():
                    down.wait_send()

    def w3_copy(n, way):
        block = W.at[:, blocks(n), quarter(x)]
        return remote(block, block, w3_send.at[n, way], w3_recv.at[n, way], at((x + (1, 3)[way]) % NX, z), v)

    def gather_x(n):
        for j in range(O):
            arrived(W.at[j, blocks(n), quarter(x)], w2_recv.at[n, j])
        for way in range(2):
            w3_copy(n, way).start()

    def w3_forward(n, way):
        block = W.at[pl.ds(4 * way, 4), blocks(n), quarter((x + (3, 1)[way]) % NX)]
        return remote(block, block, w3f_send.at[n, way], w3f_recv.at[n, way], at((x + (1, 3)[way]) % NX, z), v)

    def forward_x(n):
        for way in range(2):
            arrived(W.at[:, blocks(n), quarter((x + (3, 1)[way]) % NX)], w3_recv.at[n, way])
            w3_forward(n, way).start()

    def gathered_x(n):
        for way in range(2):
            arrived(W.at[pl.ds(4 * way, 4), blocks(n), quarter((x + 2) % NX)], w3f_recv.at[n, way])

    g_lo = ((y + 3) % NY) * 2
    g_hi = ((y + 1) % NY) * 2 + 1

    def f_copy(i):
        g, dy = ((g_lo, 1), (g_hi, 3))[i]
        return remote(R.at[g], R.at[g], f_send.at[i], a_recv.at[g], pair, ((y + dy) % NY) * 2 + core)

    def cycle_part(part):
        def body(i, carry):
            r = part * 2 + i
            row = pl.ds(pl.multiple_of(r * BV, BV), BV)
            for q in range(NV):
                mine = R[q, row, :].astype(F32)
                other = R[r, q * BV:(q + 1) * BV, :].astype(F32)
                cyc[core, row, q * BV:(q + 1) * BV] = (2.0 * mine - other.T).astype(BF)
            return carry

        lax.fori_loop(0, 2, body, 0)
        y_copy(part).start()

    def y_copy(part):
        rows = pl.ds(part * 256, 256)
        return remote(
            cyc.at[core, rows], cyc.at[core, rows], y_send.at[part], y_recv.at[part], pair, sibling
        )

    irreps = vir_ref[...]
    begin = [jnp.sum((irreps < alpha).astype(jnp.int32)) for alpha in range(1, O)]
    begin = [jnp.int32(0)] + begin + [jnp.int32(V)]

    def tables():
        good = jnp.int32(1)
        for alpha in range(O):
            first = jnp.minimum(lax.shift_right_logical(begin[alpha], 3), (V - CAP) // 8)
            st[alpha] = first
            good = jnp.where(begin[alpha + 1] - first * 8 <= CAP, good, 0)
        fits_ref[0] = good
        target = jnp.bitwise_xor(occ_ref[pair // O], occ_ref[pair % O])
        columns = jnp.bitwise_xor(jnp.broadcast_to(vir_ref[pl.ds(v, 1), :], (BV, BV)), target)
        row = lax.broadcasted_iota(jnp.int32, (BV, BV), 0)

        def body(i, carry):
            own = jnp.zeros((BV, BV), jnp.int32)
            for alpha in range(1, O):
                own = own + (row + i * BV >= begin[alpha]).astype(jnp.int32)
            key[pl.ds(pl.multiple_of(i * BV, BV), BV), :] = jnp.where(own == columns, own, -1)
            return carry

        lax.fori_loop(0, V // BV, body, 0)

    def product(n, s):
        g = chunk(n)
        weights = jnp.concatenate(
            [W[O - 1 - s, blocks(n)].reshape(GW, BV), W[s, blocks(n)].reshape(GW, BV)], axis=1
        )
        columns = pl.ds(pl.multiple_of(g * GW, GW), GW)

        def body(xx, carry):
            for m in range(4):
                value = jnp.dot(
                    cyc[xx, pl.ds(m * 256, 256), columns], weights, preferred_element_type=F32
                )
                for side in range(2):
                    j = (O - 1 - s, s)[side]
                    rows = pl.ds(pl.multiple_of((j * 2 + xx) * V + m * 256, 256), 256)
                    part = value[:, side * BV:(side + 1) * BV]
                    C[rows, :] = part if n == 0 else C[rows, :] + part
            return carry

        lax.fori_loop(0, 2, body, 0)

    def products(n):
        def body(s, carry):
            product(n, s)
            return carry

        lax.fori_loop(0, 4, body, 0)

    move_z(0)
    a_sibling().start()
    for cc in range(2):
        for dy in (1, 3):
            a_copy(dy, cc).start()
    tables()
    left_z(0)
    move_z(1)
    a_arrived(g_lo)
    f_copy(0).start()
    a_arrived(g_hi)
    f_copy(1).start()
    gather_x(0)
    left_z(1)
    move_z(2)
    forward_x(0)
    gather_x(1)
    left_z(2)
    move_z(3)
    a_arrived(v)
    a_arrived(sibling)
    a_arrived(g_lo + 1)
    a_arrived(g_hi - 1)
    a_arrived(((y + 2) % NY) * 2)
    a_arrived(((y + 2) % NY) * 2 + 1)
    cycle_part(0)
    cycle_part(1)
    forward_x(1)
    gather_x(2)
    cycle_part(2)
    cycle_part(3)
    forward_x(2)
    gathered_x(0)
    for part in range(4):
        arrived(cyc.at[1 - core, pl.ds(part * 256, 256)], y_recv.at[part])
    products(0)
    gather_x(3)
    gathered_x(1)
    products(1)
    forward_x(3)
    gathered_x(2)
    products(2)
    gathered_x(3)

    colb = jnp.broadcast_to(vir_ref[pl.ds(v, 1), :], (CAP, BV))
    occ_left = occ_ref[pair // O]

    def pack(s):
        for side in range(2):
            j = (O - 1 - s, s)[side]
            target = jnp.bitwise_xor(occ_left, occ_ref[j])
            for xx in range(2):
                acc = jnp.zeros((CAP, BV), F32)
                for beta in range(O):
                    start = st[jnp.bitwise_xor(target, beta)] * 8 + (j * 2 + xx) * V
                    acc = jnp.where(colb == beta, C[pl.ds(start, CAP), :], acc)
                Pk[j, xx] = acc.astype(BF)

    def hop(buf, send, recv, j, c, step):
        piece = buf.at[j, c // NP, pl.ds((c % NP) * PR, PR)]
        return remote(piece, piece, send.at[j, c], recv.at[j, c], at(x, z + step), v)

    def flow(buf, send, recv, j, c, step, first):
        rows = pl.ds((c % NP) * PR, PR)

        @pl.when(first)
        def _():
            buf[j, c // NP, rows] = Pk[j, c // NP, rows]

        @pl.when(jnp.logical_not(first))
        def _():
            hop(buf, send, recv, j, c, step).wait_recv()
            buf[j, c // NP, rows] = (
                buf[j, c // NP, rows].astype(F32) + Pk[j, c // NP, rows].astype(F32)
            ).astype(BF)

        hop(buf, send, recv, j, c, step).start()

    def tick(tau, carry):
        @pl.when(tau < 4)
        def _():
            product(NG - 1, tau)
            pack(tau)

        for c in range(2 * NP):
            @pl.when(tau >= l)
            def _():
                flow(U, u_send, u_recv, O - 1 + l - tau, c, 1, l == 0)

            @pl.when(tau >= O - 1 - l)
            def _():
                flow(D, d_send, d_recv, l - (O - 1 - tau), c, -1, l == O - 1)

        return carry

    lax.fori_loop(0, O - 1, tick, 0)

    for xx in range(2):
        mid = pl.ds(xx * FR + PAD, CAP)
        Fin[mid, :] = Pk[l, xx].astype(F32)

        @pl.when(l > 0)
        def _():
            for c in range(NP):
                hop(U, u_send, u_recv, l, xx * NP + c, 1).wait_recv()
            Fin[mid, :] += U[l, xx].astype(F32)

        @pl.when(l < O - 1)
        def _():
            for c in range(NP):
                hop(D, d_send, d_recv, l, xx * NP + c, -1).wait_recv()
            Fin[mid, :] += D[l, xx].astype(F32)

        def unpack(i, carry):
            rows = pl.ds(pl.multiple_of(i * PAD, PAD), PAD)
            held = key[rows, :]
            acc = jnp.zeros((PAD, BV), F32)
            for alpha in range(O):
                first = jnp.clip(i * (PAD // 8) - st[alpha], -PAD // 8, CAP // 8) + PAD // 8
                acc = jnp.where(held == alpha, Fin[pl.ds(first * 8 + xx * FR, PAD), :], acc)
            out_ref[xx, 0, rows, :] = acc.astype(BF)
            return carry

        lax.fori_loop(0, V // PAD, unpack, 0)

    for which in spread[1:]:
        s_copy(*which).wait_send()
    a_sibling().wait_send()
    for cc in range(2):
        for dy in (1, 3):
            a_copy(dy, cc).wait_send()
    for i in range(2):
        f_copy(i).wait_send()
    for n in range(NG):
        if n == NG - 1:
            left_z(n)
        for way in range(2):
            w3_copy(n, way).wait_send()
            w3_forward(n, way).wait_send()
    for part in range(4):
        y_copy(part).wait_send()

    def drain(j, carry):
        for c in range(2 * NP):
            @pl.when(j > l)
            def _():
                hop(U, u_send, u_recv, j, c, 1).wait_send()

            @pl.when(j < l)
            def _():
                hop(D, d_send, d_recv, j, c, -1).wait_send()

        return carry

    lax.fori_loop(0, O, drain, 0)


def packed(amplitudes, w_ovvo, occ_irreps, vir_irreps):
    smem = pl.BlockSpec(memory_space=pltpu.SMEM)
    vmem = pl.BlockSpec(memory_space=pltpu.VMEM)
    anym = pl.BlockSpec(memory_space=pl.ANY)
    dma = pltpu.SemaphoreType.DMA
    return pl.pallas_call(
        packed_kernel,
        out_shape=(jax.ShapeDtypeStruct((2, 1, V, BV), BF), jax.ShapeDtypeStruct((1,), jnp.int32)),
        in_specs=[smem, vmem, anym, anym],
        out_specs=(vmem, smem),
        scratch_shapes=[
            pltpu.VMEM((NX, NV, BV // NX, BV), BF),
            pltpu.VMEM((O, NV, BV, BV), BF),
            pltpu.VMEM((NV, V, BV), BF),
            pltpu.VMEM((2, V, V), BF),
            pltpu.VMEM((O * 2 * V, BV), F32),
            pltpu.VMEM((O, 2, CAP, BV), BF),
            pltpu.VMEM((O, 2, CAP, BV), BF),
            pltpu.VMEM((O, 2, CAP, BV), BF),
            pltpu.VMEM((2 * FR, BV), F32),
            pltpu.VMEM((V, BV), jnp.int32),
            pltpu.SMEM((O,), jnp.int32),
            dma((5,)), dma((NV,)), dma((2,)), dma((NG, 2, NX)), dma((NX, NV)),
            dma((NG, 4, 2)), dma((NG, O)), dma((NG, 2)), dma((NG, 2)), dma((NG, 2)), dma((NG, 2)), dma((4,)), dma((4,)),
            dma((O, 2 * NP)), dma((O, 2 * NP)), dma((O, 2 * NP)), dma((O, 2 * NP)),
        ],
        compiler_params=pltpu.CompilerParams(
            collective_id=0, has_side_effects=True, vmem_limit_bytes=48 * 2**20
        ),
        name="packed_cycle",
    )(occ_irreps, vir_irreps.reshape(V // BV, BV), amplitudes, w_ovvo)


def shards(amplitudes, w_ovvo, occ_irreps, vir_irreps):
    result, fits = packed(amplitudes, w_ovvo, occ_irreps, vir_irreps)
    return lax.cond(
        fits[0] == 1,
        lambda: result,
        lambda: general(amplitudes, w_ovvo, occ_irreps, vir_irreps)[:, None],
    )


def solution(mesh):
    in_specs = (P(None, "pair", None, "virt"), P("pair", "virt", None), P(), P())
    out_specs = P(None, "pair", None, "virt")
    return jax.shard_map(shards, mesh=mesh, in_specs=in_specs, out_specs=out_specs, check_vma=False)
```

```python
import functools
import math

import jax
import jax.numpy as jnp
from jax import lax
from jax.experimental import pallas as pl
from jax.experimental.pallas import tpu as pltpu
from jax.sharding import PartitionSpec as P

MESH = pl.DeviceIdType.MESH
BF = jnp.bfloat16
F32 = jnp.float32

NX, NZ, NY = 4, 16, 4
O = 8
NV = 8
V = 1024
BV = 128
CAP = 272


def swapped(block, axis, stride):
    count = lax.axis_size(axis)
    route = []
    for low in range(count):
        high = low | 1 << stride
        if high != low and high < count:
            route += [(low, high), (high, low)]
    return lax.ppermute(block, axis, route)


def bit_of(position, level):
    return position // 2**level % 2


def general(amplitudes, w_ovvo, occ_irreps, vir_irreps):
    own_tile = amplitudes[:, 0]
    devices = lax.axis_size("pair")
    tiles_side = math.isqrt(devices)
    bit_count = tiles_side.bit_length() - 1
    position = lax.axis_index("pair")
    spread = lax.all_to_all(own_tile[None], "pair", split_axis=2, concat_axis=0, tiled=True)
    shape_rest = spread.shape[1:]
    spread = spread.reshape((tiles_side, tiles_side) + shape_rest)
    spread = jnp.swapaxes(spread, 0, 1).reshape((devices,) + shape_rest)
    mirrored = lax.all_to_all(spread, "pair", split_axis=0, concat_axis=2, tiled=True)[0]
    cycle_tile = (2.0 * own_tile.astype(F32) - mirrored.astype(F32)).astype(BF)
    cycle_stack = cycle_tile[None]
    for level in range(bit_count):
        partner = swapped(cycle_stack, "pair", level)
        lower_half = bit_of(position, level) == 0
        cycle_stack = jnp.where(
            lower_half,
            jnp.concatenate([cycle_stack, partner], axis=0),
            jnp.concatenate([partner, cycle_stack], axis=0),
        )
    weight_stack = w_ovvo
    for level in range(bit_count):
        partner = swapped(weight_stack, "pair", level + bit_count)
        lower_half = bit_of(position, level + bit_count) == 0
        weight_stack = jnp.where(
            lower_half,
            jnp.concatenate([weight_stack, partner], axis=0),
            jnp.concatenate([partner, weight_stack], axis=0),
        )
    partial_value = jnp.einsum(
        "kxac,kcb->xab", cycle_stack, weight_stack, preferred_element_type=F32
    )
    pieces = lax.all_to_all(
        partial_value.astype(BF)[None], "virt", split_axis=3, concat_axis=0, tiled=True
    )
    summed = jnp.sum(pieces.astype(F32), axis=0)
    width_local = summed.shape[2]
    occ_order = jnp.arange(occ_irreps.shape[0], dtype=jnp.int32)
    left_irrep = jnp.sum(jnp.where(occ_order == position // tiles_side, occ_irreps, 0))
    right_irrep = jnp.sum(jnp.where(occ_order == position % tiles_side, occ_irreps, 0))
    column_irreps = lax.dynamic_slice_in_dim(
        vir_irreps, lax.axis_index("virt") * width_local, width_local
    )
    target = jnp.bitwise_xor(left_irrep, right_irrep)
    allowed = jnp.bitwise_xor(vir_irreps[:, None], column_irreps[None, :]) == target
    return jnp.where(allowed[None], summed, 0.0).astype(BF)


PAD = 32
FR = CAP + 2 * PAD
NG = 4
PIECES = ((0, 144), (144, 128))
NP = len(PIECES)
GW = V // NG


def packed_kernel(
    occ_ref, vir_ref, amp_ref, w_ref, out_ref, fits_ref,
    S, W, R, cyc, C, Pk, U, D, Fin, key, st,
    a_send, a_recv, f_send, s_send, s_recv,
    w2_send, w2_recv, p_send, p_recv, pf_send, pf_recv, w3_send, w3_recv, w3f_send, w3f_recv, y_send, y_recv,
    u_send, u_recv, d_send, d_recv,
):
    pair, v = lax.axis_index("pair"), lax.axis_index("virt")
    x, z = pair // NZ, pair % NZ
    half, l = z // O, z % O
    y, core = v // 2, v % 2
    sibling = v + 1 - 2 * core

    def remote(src, dst, send, recv, p, q):
        return pltpu.make_async_remote_copy(
            src_ref=src, dst_ref=dst, send_sem=send, recv_sem=recv,
            device_id=(p, q), device_id_type=MESH,
        )

    def arrived(block, sem):
        pltpu.make_async_copy(block, block, sem).wait()

    def at(px, pz):
        return px * NZ + pz

    bar = pltpu.get_barrier_semaphore()

    def greet(p, q):
        pl.semaphore_signal(bar, inc=1, device_id=(p, q), device_id_type=MESH)

    for d in range(1, NX * NV):
        greet(at((x + d // NV) % NX, z), (v + d) % NV)
    for j in range(O):
        source = O * (l % 2) + j

        @pl.when(source != z)
        def _():
            greet(at(x, source), v)

    @pl.when(l > 0)
    def _():
        greet(at(x, z - 1), v)

    @pl.when(l < O - 1)
    def _():
        greet(at(x, z + 1), v)

    own_k = (l % 2 == half).astype(jnp.int32)
    ends = (l > 0).astype(jnp.int32) + (l < O - 1).astype(jnp.int32)
    pl.semaphore_wait(bar, NX * NV - 1 + O - own_k + ends)

    XR = BV // NX

    def chunk(n):
        return (y + n) % NY

    def blocks(n):
        return pl.ds(2 * chunk(n), 2)

    def quarter(q):
        return pl.ds(pl.multiple_of(q * XR, XR), XR)

    def s_copy(n, c, d):
        p, q = (x + d) % NX, ((y - n + NY) % NY) * 2 + (core + c) % 2
        src = w_ref.at[0, quarter(p), pl.ds(pl.multiple_of(q * BV, BV), BV)]
        if n + c + d == 0:
            return pltpu.make_async_copy(src, S.at[x, v], s_recv.at[x, v])
        return remote(src, S.at[x, v], s_send.at[n, c, d], s_recv.at[x, v], at(p, z), q)

    spread = [(n, c, d) for n in range(NG) for c in range(2) for d in range(NX)]
    for which in spread:
        s_copy(*which).start()

    a_local = pltpu.make_async_copy(amp_ref.at[core, 0], R.at[v], a_recv.at[v])
    a_local.start()

    def a_sibling():
        return remote(amp_ref.at[1 - core, 0], R.at[v], a_send.at[4], a_recv.at[v], pair, sibling)

    def a_copy(dy, cc):
        return remote(
            amp_ref.at[cc, 0], R.at[v], a_send.at[(dy // 2) * 2 + cc], a_recv.at[v],
            pair, ((y + dy) % NY) * 2 + cc,
        )

    def a_arrived(g):
        arrived(R.at[g], a_recv.at[g])

    odd = (half + l) % 2

    def w2_copy(n, slot, way):
        hops = 2 * slot + 2 - odd
        step = (hops, -hops)[way]
        q = ((l + step + O) % O) // 2
        src, dst = S.at[q, blocks(n)], W.at[l, blocks(n), quarter(x)]
        dz = (z + step + NZ) % NZ
        return src, dst, remote(src, dst, w2_send.at[n, slot, way], w2_recv.at[n, l], at(x, dz), v)

    def move_z(n):
        for q in range(NX):
            for c in range(2):
                g = 2 * chunk(n) + c
                arrived(S.at[q, g], s_recv.at[q, g])
        for slot in (3, 2, 1, 0):
            src, dst, up = w2_copy(n, slot, 0)
            up.start()
            src, dst, down = w2_copy(n, slot, 1)
            if slot < 3:
                down.start()
            else:
                @pl.when(odd == 1)
                def _():
                    down.start()

                @pl.when(odd == 0)
                def _():
                    pltpu.make_async_copy(src, dst, w2_recv.at[n, l]).start()

    def left_z(n):
        for slot in (3, 2, 1, 0):
            w2_copy(n, slot, 0)[2].wait_send()
            down = w2_copy(n, slot, 1)[2]
            if slot < 3:
                down.wait_send()
            else:
                @pl.when(odd == 1)
                def _():
                    down.wait_send()

    def w3_copy(n, way):
        block = W.at[:, blocks(n), quarter(x)]
        return remote(block, block, w3_send.at[n, way], w3_recv.at[n, way], at((x + (1, 3)[way]) % NX, z), v)

    def gather_x(n):
        for j in range(O):
            arrived(W.at[j, blocks(n), quarter(x)], w2_recv.at[n, j])
        for way in range(2):
            w3_copy(n, way).start()

    def w3_forward(n, way):
        block = W.at[pl.ds(4 * way, 4), blocks(n), quarter((x + (3, 1)[way]) % NX)]
        return remote(block, block, w3f_send.at[n, way], w3f_recv.at[n, way], at((x + (1, 3)[way]) % NX, z), v)

    LAST = NG - 1

    def pair_copy(j, way):
        block = W.at[j, blocks(LAST), quarter(x)]
        return remote(block, block, p_send.at[j, way], p_recv.at[j, way], at((x + (1, 3)[way]) % NX, z), v)

    def pair_forward(j, way):
        block = W.at[j, blocks(LAST), quarter((x + (3, 1)[way]) % NX)]
        return remote(block, block, pf_send.at[j], pf_recv.at[j], at((x + (1, 3)[way]) % NX, z), v)

    def gather_pair(s):
        for j in (s, O - 1 - s):
            arrived(W.at[j, blocks(LAST), quarter(x)], w2_recv.at[LAST, j])
            for way in range(2):
                pair_copy(j, way).start()

    def forward_pair(s):
        for way, j in enumerate((s, O - 1 - s)):
            arrived(W.at[j, blocks(LAST), quarter((x + (3, 1)[way]) % NX)], p_recv.at[j, way])
            pair_forward(j, way).start()

    def gathered_pair(s):
        for way, j in enumerate((s, O - 1 - s)):
            arrived(W.at[j, blocks(LAST), quarter((x + (1, 3)[way]) % NX)], p_recv.at[j, 1 - way])
            arrived(W.at[j, blocks(LAST), quarter((x + 2) % NX)], pf_recv.at[j])

    def forward_x(n):
        for way in range(2):
            arrived(W.at[:, blocks(n), quarter((x + (3, 1)[way]) % NX)], w3_recv.at[n, way])
            w3_forward(n, way).start()

    def gathered_x(n):
        for way in range(2):
            arrived(W.at[pl.ds(4 * way, 4), blocks(n), quarter((x + 2) % NX)], w3f_recv.at[n, way])

    g_lo = ((y + 3) % NY) * 2
    g_hi = ((y + 1) % NY) * 2 + 1

    def f_copy(i):
        g, dy = ((g_lo, 1), (g_hi, 3))[i]
        return remote(R.at[g], R.at[g], f_send.at[i], a_recv.at[g], pair, ((y + dy) % NY) * 2 + core)

    def place(e, i):
        return ((y + e) % NY) * 2 + i

    FIRST = [(e, i) for e in (0, 1, 3) for i in range(2)]
    LATE = [(2, i) for i in range(2)]

    def cycle_rows(r, columns):
        row = pl.ds(pl.multiple_of(r * BV, BV), BV)
        for which in columns:
            q = place(*which)
            column = pl.ds(pl.multiple_of(q * BV, BV), BV)
            other = R[r, column, :].astype(F32)
            cyc[core, row, column] = (2.0 * R[q, row, :].astype(F32) - other.T).astype(BF)

    def cycle_chip(e, columns):
        def body(i, carry):
            cycle_rows(place(e, i), columns)
            return carry

        lax.fori_loop(0, 2, body, 0)

    def y_copy(e):
        part = (y + e) % NY
        rows = pl.ds(pl.multiple_of(part * 256, 256), 256)
        return remote(
            cyc.at[core, rows], cyc.at[core, rows], y_send.at[part], y_recv.at[part], pair, sibling
        )

    irreps = vir_ref[...]
    begin = [jnp.sum((irreps < alpha).astype(jnp.int32)) for alpha in range(1, O)]
    begin = [jnp.int32(0)] + begin + [jnp.int32(V)]

    def tables():
        good = jnp.int32(1)
        for alpha in range(O):
            first = jnp.minimum(lax.shift_right_logical(begin[alpha], 3), (V - CAP) // 8)
            st[alpha] = first
            good = jnp.where(begin[alpha + 1] - first * 8 <= CAP, good, 0)
        fits_ref[0] = good
        target = jnp.bitwise_xor(occ_ref[pair // O], occ_ref[pair % O])
        columns = jnp.bitwise_xor(jnp.broadcast_to(vir_ref[pl.ds(v, 1), :], (BV, BV)), target)
        row = lax.broadcasted_iota(jnp.int32, (BV, BV), 0)

        def body(i, carry):
            own = jnp.zeros((BV, BV), jnp.int32)
            for alpha in range(1, O):
                own = own + (row + i * BV >= begin[alpha]).astype(jnp.int32)
            key[pl.ds(pl.multiple_of(i * BV, BV), BV), :] = jnp.where(own == columns, own, -1)
            return carry

        lax.fori_loop(0, V // BV, body, 0)

    def product(chunks, s, first):
        weights = jnp.concatenate([
            jnp.concatenate([W[j, blocks(n)].reshape(2 * BV, BV) for n in chunks], axis=0)
            for j in (O - 1 - s, s)
        ], axis=1)

        def body(xx, carry):
            for m in range(4):
                rows = pl.ds(m * 256, 256)
                left = jnp.concatenate([
                    cyc[xx, rows, pl.ds(pl.multiple_of(chunk(n) * 256, 256), 256)] for n in chunks
                ], axis=1)
                value = jnp.dot(left, weights, preferred_element_type=F32)
                for side in range(2):
                    j = (O - 1 - s, s)[side]
                    rows = pl.ds(pl.multiple_of((j * 2 + xx) * V + m * 256, 256), 256)
                    part = value[:, side * BV:(side + 1) * BV]
                    C[rows, :] = part if first else C[rows, :] + part
            return carry

        lax.fori_loop(0, 2, body, 0)

    a_sibling().start()
    for cc in range(2):
        for dy in (1, 3):
            a_copy(dy, cc).start()
    move_z(0)
    tables()
    left_z(0)
    move_z(1)
    a_arrived(g_lo)
    f_copy(0).start()
    a_arrived(g_hi)
    f_copy(1).start()
    gather_x(0)
    left_z(1)
    move_z(2)
    forward_x(0)
    gather_x(1)
    left_z(2)
    move_z(3)
    a_arrived(v)
    a_arrived(sibling)
    a_arrived(g_lo + 1)
    a_arrived(g_hi - 1)
    for e in (0, 1, 3):
        cycle_chip(e, FIRST)
    forward_x(1)
    a_arrived(((y + 2) % NY) * 2)
    a_arrived(((y + 2) % NY) * 2 + 1)
    for e in (0, 1, 3):
        cycle_chip(e, LATE)
        y_copy(e).start()
    gather_x(2)
    cycle_chip(2, FIRST + LATE)
    y_copy(2).start()
    forward_x(2)
    gathered_x(0)
    for part in range(4):
        arrived(cyc.at[1 - core, pl.ds(part * 256, 256)], y_recv.at[part])
    for s in range(4):
        gather_pair(s)
    gathered_x(1)
    gathered_x(2)
    for s in range(4):
        product((0, 1, 2), s, True)
        if s == 1:
            for r in range(4):
                forward_pair(r)

    colb = jnp.broadcast_to(vir_ref[pl.ds(v, 1), :], (CAP, BV))
    occ_left = occ_ref[pair // O]

    def pack(s):
        for side in range(2):
            j = (O - 1 - s, s)[side]
            target = jnp.bitwise_xor(occ_left, occ_ref[j])
            for xx in range(2):
                acc = jnp.zeros((CAP, BV), F32)
                for beta in range(O):
                    start = st[jnp.bitwise_xor(target, beta)] * 8 + (j * 2 + xx) * V
                    acc = jnp.where(colb == beta, C[pl.ds(start, CAP), :], acc)
                Pk[j, xx] = acc.astype(BF)

    def hop(buf, send, recv, j, c, step):
        piece = buf.at[j, c // NP, pl.ds(*PIECES[c % NP])]
        return remote(piece, piece, send.at[j, c], recv.at[j, c], at(x, z + step), v)

    def flow(buf, send, recv, j, c, step, first):
        rows = pl.ds(*PIECES[c % NP])

        @pl.when(first)
        def _():
            buf[j, c // NP, rows] = Pk[j, c // NP, rows]

        @pl.when(jnp.logical_not(first))
        def _():
            hop(buf, send, recv, j, c, step).wait_recv()
            buf[j, c // NP, rows] = (
                buf[j, c // NP, rows].astype(F32) + Pk[j, c // NP, rows].astype(F32)
            ).astype(BF)

        hop(buf, send, recv, j, c, step).start()

    def tick(tau, carry):
        if isinstance(tau, int):
            gathered_pair(tau)
            product((LAST,), tau, False)
            pack(tau)

        for c in range(2 * NP):
            @pl.when(tau >= l)
            def _():
                flow(U, u_send, u_recv, O - 1 + l - tau, c, 1, l == 0)

            @pl.when(tau >= O - 1 - l)
            def _():
                flow(D, d_send, d_recv, l - (O - 1 - tau), c, -1, l == O - 1)

        return carry

    for tau in range(4):
        tick(tau, 0)
    lax.fori_loop(4, O - 1, tick, 0)

    for xx in range(2):
        mid = pl.ds(xx * FR + PAD, CAP)
        Fin[mid, :] = Pk[l, xx].astype(F32)

        @pl.when(l > 0)
        def _():
            for c in range(NP):
                hop(U, u_send, u_recv, l, xx * NP + c, 1).wait_recv()
            Fin[mid, :] += U[l, xx].astype(F32)

        @pl.when(l < O - 1)
        def _():
            for c in range(NP):
                hop(D, d_send, d_recv, l, xx * NP + c, -1).wait_recv()
            Fin[mid, :] += D[l, xx].astype(F32)

        def unpack(i, carry):
            rows = pl.ds(pl.multiple_of(i * PAD, PAD), PAD)
            held = key[rows, :]
            acc = jnp.zeros((PAD, BV), F32)
            for alpha in range(O):
                first = jnp.clip(i * (PAD // 8) - st[alpha], -PAD // 8, CAP // 8) + PAD // 8
                acc = jnp.where(held == alpha, Fin[pl.ds(first * 8 + xx * FR, PAD), :], acc)
            out_ref[xx, 0, rows, :] = acc.astype(BF)
            return carry

        lax.fori_loop(0, V // PAD, unpack, 0)

    for which in spread[1:]:
        s_copy(*which).wait_send()
    a_sibling().wait_send()
    for cc in range(2):
        for dy in (1, 3):
            a_copy(dy, cc).wait_send()
    for i in range(2):
        f_copy(i).wait_send()
    for n in range(NG):
        if n == NG - 1:
            left_z(n)
        for way in range(2) if n < LAST else ():
            w3_copy(n, way).wait_send()
            w3_forward(n, way).wait_send()
    for j in range(O):
        for way in range(2):
            pair_copy(j, way).wait_send()
        pair_forward(j, j // 4).wait_send()
    for part in range(4):
        y_copy(part).wait_send()

    def drain(j, carry):
        for c in range(2 * NP):
            @pl.when(j > l)
            def _():
                hop(U, u_send, u_recv, j, c, 1).wait_send()

            @pl.when(j < l)
            def _():
                hop(D, d_send, d_recv, j, c, -1).wait_send()

        return carry

    lax.fori_loop(0, O, drain, 0)


def packed(amplitudes, w_ovvo, occ_irreps, vir_irreps):
    smem = pl.BlockSpec(memory_space=pltpu.SMEM)
    vmem = pl.BlockSpec(memory_space=pltpu.VMEM)
    anym = pl.BlockSpec(memory_space=pl.ANY)
    dma = pltpu.SemaphoreType.DMA
    return pl.pallas_call(
        packed_kernel,
        out_shape=(jax.ShapeDtypeStruct((2, 1, V, BV), BF), jax.ShapeDtypeStruct((1,), jnp.int32)),
        in_specs=[smem, vmem, anym, anym],
        out_specs=(vmem, smem),
        scratch_shapes=[
            pltpu.VMEM((NX, NV, BV // NX, BV), BF),
            pltpu.VMEM((O, NV, BV, BV), BF),
            pltpu.VMEM((NV, V, BV), BF),
            pltpu.VMEM((2, V, V), BF),
            pltpu.VMEM((O * 2 * V, BV), F32),
            pltpu.VMEM((O, 2, CAP, BV), BF),
            pltpu.VMEM((O, 2, CAP, BV), BF),
            pltpu.VMEM((O, 2, CAP, BV), BF),
            pltpu.VMEM((2 * FR, BV), F32),
            pltpu.VMEM((V, BV), jnp.int32),
            pltpu.SMEM((O,), jnp.int32),
            dma((5,)), dma((NV,)), dma((2,)), dma((NG, 2, NX)), dma((NX, NV)),
            dma((NG, 4, 2)), dma((NG, O)), dma((O, 2)), dma((O, 2)), dma((O,)), dma((O,)), dma((NG, 2)), dma((NG, 2)), dma((NG, 2)), dma((NG, 2)), dma((4,)), dma((4,)),
            dma((O, 2 * NP)), dma((O, 2 * NP)), dma((O, 2 * NP)), dma((O, 2 * NP)),
        ],
        compiler_params=pltpu.CompilerParams(
            collective_id=0, has_side_effects=True, vmem_limit_bytes=48 * 2**20
        ),
        name="packed_cycle",
    )(occ_irreps, vir_irreps.reshape(V // BV, BV), amplitudes, w_ovvo)


def shards(amplitudes, w_ovvo, occ_irreps, vir_irreps):
    result, fits = packed(amplitudes, w_ovvo, occ_irreps, vir_irreps)
    return lax.cond(
        fits[0] == 1,
        lambda: result,
        lambda: general(amplitudes, w_ovvo, occ_irreps, vir_irreps)[:, None],
    )


def solution(mesh):
    in_specs = (P(None, "pair", None, "virt"), P("pair", "virt", None), P(), P())
    out_specs = P(None, "pair", None, "virt")
    return jax.shard_map(shards, mesh=mesh, in_specs=in_specs, out_specs=out_specs, check_vma=False)
```

```python
import functools
import math

import jax
import jax.numpy as jnp
from jax import lax
from jax.experimental import pallas as pl
from jax.experimental.pallas import tpu as pltpu
from jax.sharding import PartitionSpec as P

MESH = pl.DeviceIdType.MESH
BF = jnp.bfloat16
F32 = jnp.float32

NX, NZ, NY = 4, 16, 4
O = 8
NV = 8
V = 1024
BV = 128
CAP = 272


def swapped(block, axis, stride):
    count = lax.axis_size(axis)
    route = []
    for low in range(count):
        high = low | 1 << stride
        if high != low and high < count:
            route += [(low, high), (high, low)]
    return lax.ppermute(block, axis, route)


def bit_of(position, level):
    return position // 2**level % 2


def general(amplitudes, w_ovvo, occ_irreps, vir_irreps):
    own_tile = amplitudes[:, 0]
    devices = lax.axis_size("pair")
    tiles_side = math.isqrt(devices)
    bit_count = tiles_side.bit_length() - 1
    position = lax.axis_index("pair")
    spread = lax.all_to_all(own_tile[None], "pair", split_axis=2, concat_axis=0, tiled=True)
    shape_rest = spread.shape[1:]
    spread = spread.reshape((tiles_side, tiles_side) + shape_rest)
    spread = jnp.swapaxes(spread, 0, 1).reshape((devices,) + shape_rest)
    mirrored = lax.all_to_all(spread, "pair", split_axis=0, concat_axis=2, tiled=True)[0]
    cycle_tile = (2.0 * own_tile.astype(F32) - mirrored.astype(F32)).astype(BF)
    cycle_stack = cycle_tile[None]
    for level in range(bit_count):
        partner = swapped(cycle_stack, "pair", level)
        lower_half = bit_of(position, level) == 0
        cycle_stack = jnp.where(
            lower_half,
            jnp.concatenate([cycle_stack, partner], axis=0),
            jnp.concatenate([partner, cycle_stack], axis=0),
        )
    weight_stack = w_ovvo
    for level in range(bit_count):
        partner = swapped(weight_stack, "pair", level + bit_count)
        lower_half = bit_of(position, level + bit_count) == 0
        weight_stack = jnp.where(
            lower_half,
            jnp.concatenate([weight_stack, partner], axis=0),
            jnp.concatenate([partner, weight_stack], axis=0),
        )
    partial_value = jnp.einsum(
        "kxac,kcb->xab", cycle_stack, weight_stack, preferred_element_type=F32
    )
    pieces = lax.all_to_all(
        partial_value.astype(BF)[None], "virt", split_axis=3, concat_axis=0, tiled=True
    )
    summed = jnp.sum(pieces.astype(F32), axis=0)
    width_local = summed.shape[2]
    occ_order = jnp.arange(occ_irreps.shape[0], dtype=jnp.int32)
    left_irrep = jnp.sum(jnp.where(occ_order == position // tiles_side, occ_irreps, 0))
    right_irrep = jnp.sum(jnp.where(occ_order == position % tiles_side, occ_irreps, 0))
    column_irreps = lax.dynamic_slice_in_dim(
        vir_irreps, lax.axis_index("virt") * width_local, width_local
    )
    target = jnp.bitwise_xor(left_irrep, right_irrep)
    allowed = jnp.bitwise_xor(vir_irreps[:, None], column_irreps[None, :]) == target
    return jnp.where(allowed[None], summed, 0.0).astype(BF)


PAD = 32
FR = CAP + 2 * PAD
NG = 4
PIECES = ((0, 144), (144, 128))
NP = len(PIECES)
GW = V // NG


def packed_kernel(
    occ_ref, vir_ref, amp_ref, w_ref, out_ref, fits_ref,
    S, W, R, cyc, C, Pk, U, D, Fin, key, st,
    a_send, a_recv, f_send, s_send, s_recv,
    w2_send, w2_recv, p_send, p_recv, pf_send, pf_recv, w3_send, w3_recv, w3f_send, w3f_recv, y_send, y_recv,
    u_send, u_recv, d_send, d_recv,
):
    pair, v = lax.axis_index("pair"), lax.axis_index("virt")
    x, z = pair // NZ, pair % NZ
    half, l = z // O, z % O
    y, core = v // 2, v % 2
    sibling = v + 1 - 2 * core

    def remote(src, dst, send, recv, p, q):
        return pltpu.make_async_remote_copy(
            src_ref=src, dst_ref=dst, send_sem=send, recv_sem=recv,
            device_id=(p, q), device_id_type=MESH,
        )

    def arrived(block, sem):
        pltpu.make_async_copy(block, block, sem).wait()

    def at(px, pz):
        return px * NZ + pz

    bar = pltpu.get_barrier_semaphore()

    def greet(p, q):
        pl.semaphore_signal(bar, inc=1, device_id=(p, q), device_id_type=MESH)

    for d in range(1, NX * NV):
        greet(at((x + d // NV) % NX, z), (v + d) % NV)
    for j in range(O):
        source = O * (l % 2) + j

        @pl.when(source != z)
        def _():
            greet(at(x, source), v)

    @pl.when(l > 0)
    def _():
        greet(at(x, z - 1), v)

    @pl.when(l < O - 1)
    def _():
        greet(at(x, z + 1), v)

    own_k = (l % 2 == half).astype(jnp.int32)
    ends = (l > 0).astype(jnp.int32) + (l < O - 1).astype(jnp.int32)
    pl.semaphore_wait(bar, NX * NV - 1 + O - own_k + ends)

    XR = BV // NX

    def chunk(n):
        return (y + n) % NY

    def blocks(n):
        return pl.ds(2 * chunk(n), 2)

    def quarter(q):
        return pl.ds(pl.multiple_of(q * XR, XR), XR)

    def s_copy(n, c, d):
        p, q = (x + d) % NX, ((y - n + NY) % NY) * 2 + (core + c) % 2
        src = w_ref.at[0, quarter(p), pl.ds(pl.multiple_of(q * BV, BV), BV)]
        if n + c + d == 0:
            return pltpu.make_async_copy(src, S.at[x, v], s_recv.at[x, v])
        return remote(src, S.at[x, v], s_send.at[n, c, d], s_recv.at[x, v], at(p, z), q)

    spread = [(n, c, d) for n in range(NG) for c in range(2) for d in range(NX)]
    for which in spread:
        s_copy(*which).start()

    a_local = pltpu.make_async_copy(amp_ref.at[core, 0], R.at[v], a_recv.at[v])
    a_local.start()

    def a_sibling():
        return remote(amp_ref.at[1 - core, 0], R.at[v], a_send.at[4], a_recv.at[v], pair, sibling)

    def a_copy(dy, cc):
        return remote(
            amp_ref.at[cc, 0], R.at[v], a_send.at[(dy // 2) * 2 + cc], a_recv.at[v],
            pair, ((y + dy) % NY) * 2 + cc,
        )

    def a_arrived(g):
        arrived(R.at[g], a_recv.at[g])

    odd = (half + l) % 2

    def w2_copy(n, slot, way):
        hops = 2 * slot + 2 - odd
        step = (hops, -hops)[way]
        q = ((l + step + O) % O) // 2
        src, dst = S.at[q, blocks(n)], W.at[l, blocks(n), quarter(x)]
        dz = (z + step + NZ) % NZ
        return src, dst, remote(src, dst, w2_send.at[n, slot, way], w2_recv.at[n, l], at(x, dz), v)

    def move_z(n):
        for q in range(NX):
            for c in range(2):
                g = 2 * chunk(n) + c
                arrived(S.at[q, g], s_recv.at[q, g])
        for slot in (3, 2, 1, 0):
            src, dst, up = w2_copy(n, slot, 0)
            up.start()
            src, dst, down = w2_copy(n, slot, 1)
            if slot < 3:
                down.start()
            else:
                @pl.when(odd == 1)
                def _():
                    down.start()

                @pl.when(odd == 0)
                def _():
                    pltpu.make_async_copy(src, dst, w2_recv.at[n, l]).start()

    def left_z(n):
        for slot in (3, 2, 1, 0):
            w2_copy(n, slot, 0)[2].wait_send()
            down = w2_copy(n, slot, 1)[2]
            if slot < 3:
                down.wait_send()
            else:
                @pl.when(odd == 1)
                def _():
                    down.wait_send()

    def w3_copy(n, way):
        block = W.at[:, blocks(n), quarter(x)]
        return remote(block, block, w3_send.at[n, way], w3_recv.at[n, way], at((x + (1, 3)[way]) % NX, z), v)

    def gather_x(n):
        for j in range(O):
            arrived(W.at[j, blocks(n), quarter(x)], w2_recv.at[n, j])
        for way in range(2):
            w3_copy(n, way).start()

    def w3_forward(n, way):
        block = W.at[pl.ds(4 * way, 4), blocks(n), quarter((x + (3, 1)[way]) % NX)]
        return remote(block, block, w3f_send.at[n, way], w3f_recv.at[n, way], at((x + (1, 3)[way]) % NX, z), v)

    LAST = NG - 1

    def pair_copy(j, way):
        block = W.at[j, blocks(LAST), quarter(x)]
        return remote(block, block, p_send.at[j, way], p_recv.at[j, way], at((x + (1, 3)[way]) % NX, z), v)

    def pair_forward(j, way):
        block = W.at[j, blocks(LAST), quarter((x + (3, 1)[way]) % NX)]
        return remote(block, block, pf_send.at[j], pf_recv.at[j], at((x + (1, 3)[way]) % NX, z), v)

    def gather_pair(s):
        for j in (s, O - 1 - s):
            arrived(W.at[j, blocks(LAST), quarter(x)], w2_recv.at[LAST, j])
            for way in range(2):
                pair_copy(j, way).start()

    def forward_pair(s):
        for way, j in enumerate((s, O - 1 - s)):
            arrived(W.at[j, blocks(LAST), quarter((x + (3, 1)[way]) % NX)], p_recv.at[j, way])
            pair_forward(j, way).start()

    def gathered_pair(s):
        for way, j in enumerate((s, O - 1 - s)):
            arrived(W.at[j, blocks(LAST), quarter((x + (1, 3)[way]) % NX)], p_recv.at[j, 1 - way])
            arrived(W.at[j, blocks(LAST), quarter((x + 2) % NX)], pf_recv.at[j])

    def forward_x(n):
        for way in range(2):
            arrived(W.at[:, blocks(n), quarter((x + (3, 1)[way]) % NX)], w3_recv.at[n, way])
            w3_forward(n, way).start()

    def gathered_x(n):
        for way in range(2):
            arrived(W.at[pl.ds(4 * way, 4), blocks(n), quarter((x + 2) % NX)], w3f_recv.at[n, way])

    g_lo = ((y + 3) % NY) * 2
    g_hi = ((y + 1) % NY) * 2 + 1

    def f_copy(i):
        g, dy = ((g_lo, 1), (g_hi, 3))[i]
        return remote(R.at[g], R.at[g], f_send.at[i], a_recv.at[g], pair, ((y + dy) % NY) * 2 + core)

    def place(e, i):
        return ((y + e) % NY) * 2 + i

    FIRST = [(e, i) for e in (0, 1, 3) for i in range(2)]
    LATE = [(2, i) for i in range(2)]

    def cycle_rows(r, columns):
        row = pl.ds(pl.multiple_of(r * BV, BV), BV)
        for which in columns:
            q = place(*which)
            column = pl.ds(pl.multiple_of(q * BV, BV), BV)
            other = R[r, column, :].astype(F32)
            cyc[core, row, column] = (2.0 * R[q, row, :].astype(F32) - other.T).astype(BF)

    def cycle_chip(e, columns):
        def body(i, carry):
            cycle_rows(place(e, i), columns)
            return carry

        lax.fori_loop(0, 2, body, 0)

    def y_copy(e):
        part = (y + e) % NY
        rows = pl.ds(pl.multiple_of(part * 256, 256), 256)
        return remote(
            cyc.at[core, rows], cyc.at[core, rows], y_send.at[part], y_recv.at[part], pair, sibling
        )

    irreps = vir_ref[...]
    begin = [jnp.sum((irreps < alpha).astype(jnp.int32)) for alpha in range(1, O)]
    begin = [jnp.int32(0)] + begin + [jnp.int32(V)]

    def tables():
        good = jnp.int32(1)
        for alpha in range(O):
            first = jnp.minimum(lax.shift_right_logical(begin[alpha], 3), (V - CAP) // 8)
            st[alpha] = first
            good = jnp.where(begin[alpha + 1] - first * 8 <= CAP, good, 0)
        fits_ref[0] = good
        target = jnp.bitwise_xor(occ_ref[pair // O], occ_ref[pair % O])
        columns = jnp.bitwise_xor(jnp.broadcast_to(vir_ref[pl.ds(v, 1), :], (BV, BV)), target)
        row = lax.broadcasted_iota(jnp.int32, (BV, BV), 0)

        def body(i, carry):
            own = jnp.zeros((BV, BV), jnp.int32)
            for alpha in range(1, O):
                own = own + (row + i * BV >= begin[alpha]).astype(jnp.int32)
            key[pl.ds(pl.multiple_of(i * BV, BV), BV), :] = jnp.where(own == columns, own, -1)
            return carry

        lax.fori_loop(0, V // BV, body, 0)

    def product(chunks, s, first):
        weights = jnp.concatenate([
            jnp.concatenate([W[j, blocks(n)].reshape(2 * BV, BV) for n in chunks], axis=0)
            for j in (O - 1 - s, s)
        ], axis=1)

        def body(xx, carry):
            for m in range(4):
                rows = pl.ds(m * 256, 256)
                left = jnp.concatenate([
                    cyc[xx, rows, pl.ds(pl.multiple_of(chunk(n) * 256, 256), 256)] for n in chunks
                ], axis=1)
                value = jnp.dot(left, weights, preferred_element_type=F32)
                for side in range(2):
                    j = (O - 1 - s, s)[side]
                    rows = pl.ds(pl.multiple_of((j * 2 + xx) * V + m * 256, 256), 256)
                    part = value[:, side * BV:(side + 1) * BV]
                    C[rows, :] = part if first else C[rows, :] + part
            return carry

        lax.fori_loop(0, 2, body, 0)

    a_sibling().start()
    for cc in range(2):
        for dy in (1, 3):
            a_copy(dy, cc).start()
    move_z(0)
    tables()
    left_z(0)
    move_z(1)
    a_arrived(g_lo)
    f_copy(0).start()
    a_arrived(g_hi)
    f_copy(1).start()
    gather_x(0)
    left_z(1)
    move_z(2)
    forward_x(0)
    gather_x(1)
    left_z(2)
    move_z(3)
    a_arrived(v)
    a_arrived(sibling)
    a_arrived(g_lo + 1)
    a_arrived(g_hi - 1)
    for e in (0, 1, 3):
        cycle_chip(e, FIRST)
    forward_x(1)
    a_arrived(((y + 2) % NY) * 2)
    a_arrived(((y + 2) % NY) * 2 + 1)
    for e in (0, 1, 3):
        cycle_chip(e, LATE)
        y_copy(e).start()
    gather_x(2)
    cycle_chip(2, FIRST + LATE)
    y_copy(2).start()
    forward_x(2)
    gathered_x(0)
    for part in range(4):
        arrived(cyc.at[1 - core, pl.ds(part * 256, 256)], y_recv.at[part])
    for s in range(4):
        gather_pair(s)
    gathered_x(1)
    gathered_x(2)
    product((0, 1, 2), 0, True)
    for s in range(4):
        forward_pair(s)
    product((0, 1, 2), 1, True)

    colb = jnp.broadcast_to(vir_ref[pl.ds(v, 1), :], (CAP, BV))
    occ_left = occ_ref[pair // O]

    def pack(s):
        for side in range(2):
            j = (O - 1 - s, s)[side]
            target = jnp.bitwise_xor(occ_left, occ_ref[j])
            for xx in range(2):
                acc = jnp.zeros((CAP, BV), F32)
                for beta in range(O):
                    start = st[jnp.bitwise_xor(target, beta)] * 8 + (j * 2 + xx) * V
                    acc = jnp.where(colb == beta, C[pl.ds(start, CAP), :], acc)
                Pk[j, xx] = acc.astype(BF)

    def hop(buf, send, recv, j, c, step):
        piece = buf.at[j, c // NP, pl.ds(*PIECES[c % NP])]
        return remote(piece, piece, send.at[j, c], recv.at[j, c], at(x, z + step), v)

    def flow(buf, send, recv, j, c, step, first):
        rows = pl.ds(*PIECES[c % NP])

        @pl.when(first)
        def _():
            buf[j, c // NP, rows] = Pk[j, c // NP, rows]

        @pl.when(jnp.logical_not(first))
        def _():
            hop(buf, send, recv, j, c, step).wait_recv()
            buf[j, c // NP, rows] = (
                buf[j, c // NP, rows].astype(F32) + Pk[j, c // NP, rows].astype(F32)
            ).astype(BF)

        hop(buf, send, recv, j, c, step).start()

    def tick(tau, carry):
        if isinstance(tau, int):
            gathered_pair(tau)
            product((LAST,), tau, False)
            pack(tau)

        for c in range(2 * NP):
            @pl.when(tau >= l)
            def _():
                flow(U, u_send, u_recv, O - 1 + l - tau, c, 1, l == 0)

            @pl.when(tau >= O - 1 - l)
            def _():
                flow(D, d_send, d_recv, l - (O - 1 - tau), c, -1, l == O - 1)

        return carry

    for tau in range(4):
        tick(tau, 0)
        if tau < 2:
            product((0, 1, 2), tau + 2, True)
    lax.fori_loop(4, O - 1, tick, 0)

    for xx in range(2):
        mid = pl.ds(xx * FR + PAD, CAP)
        Fin[mid, :] = Pk[l, xx].astype(F32)

        @pl.when(l > 0)
        def _():
            for c in range(NP):
                hop(U, u_send, u_recv, l, xx * NP + c, 1).wait_recv()
            Fin[mid, :] += U[l, xx].astype(F32)

        @pl.when(l < O - 1)
        def _():
            for c in range(NP):
                hop(D, d_send, d_recv, l, xx * NP + c, -1).wait_recv()
            Fin[mid, :] += D[l, xx].astype(F32)

        def unpack(i, carry):
            rows = pl.ds(pl.multiple_of(i * PAD, PAD), PAD)
            held = key[rows, :]
            acc = jnp.zeros((PAD, BV), F32)
            for alpha in range(O):
                first = jnp.clip(i * (PAD // 8) - st[alpha], -PAD // 8, CAP // 8) + PAD // 8
                acc = jnp.where(held == alpha, Fin[pl.ds(first * 8 + xx * FR, PAD), :], acc)
            out_ref[xx, 0, rows, :] = acc.astype(BF)
            return carry

        lax.fori_loop(0, V // PAD, unpack, 0)

    for which in spread[1:]:
        s_copy(*which).wait_send()
    a_sibling().wait_send()
    for cc in range(2):
        for dy in (1, 3):
            a_copy(dy, cc).wait_send()
    for i in range(2):
        f_copy(i).wait_send()
    for n in range(NG):
        if n == NG - 1:
            left_z(n)
        for way in range(2) if n < LAST else ():
            w3_copy(n, way).wait_send()
            w3_forward(n, way).wait_send()
    for j in range(O):
        for way in range(2):
            pair_copy(j, way).wait_send()
        pair_forward(j, j // 4).wait_send()
    for part in range(4):
        y_copy(part).wait_send()

    def drain(j, carry):
        for c in range(2 * NP):
            @pl.when(j > l)
            def _():
                hop(U, u_send, u_recv, j, c, 1).wait_send()

            @pl.when(j < l)
            def _():
                hop(D, d_send, d_recv, j, c, -1).wait_send()

        return carry

    lax.fori_loop(0, O, drain, 0)


def packed(amplitudes, w_ovvo, occ_irreps, vir_irreps):
    smem = pl.BlockSpec(memory_space=pltpu.SMEM)
    vmem = pl.BlockSpec(memory_space=pltpu.VMEM)
    anym = pl.BlockSpec(memory_space=pl.ANY)
    dma = pltpu.SemaphoreType.DMA
    return pl.pallas_call(
        packed_kernel,
        out_shape=(jax.ShapeDtypeStruct((2, 1, V, BV), BF), jax.ShapeDtypeStruct((1,), jnp.int32)),
        in_specs=[smem, vmem, anym, anym],
        out_specs=(vmem, smem),
        scratch_shapes=[
            pltpu.VMEM((NX, NV, BV // NX, BV), BF),
            pltpu.VMEM((O, NV, BV, BV), BF),
            pltpu.VMEM((NV, V, BV), BF),
            pltpu.VMEM((2, V, V), BF),
            pltpu.VMEM((O * 2 * V, BV), F32),
            pltpu.VMEM((O, 2, CAP, BV), BF),
            pltpu.VMEM((O, 2, CAP, BV), BF),
            pltpu.VMEM((O, 2, CAP, BV), BF),
            pltpu.VMEM((2 * FR, BV), F32),
            pltpu.VMEM((V, BV), jnp.int32),
            pltpu.SMEM((O,), jnp.int32),
            dma((5,)), dma((NV,)), dma((2,)), dma((NG, 2, NX)), dma((NX, NV)),
            dma((NG, 4, 2)), dma((NG, O)), dma((O, 2)), dma((O, 2)), dma((O,)), dma((O,)), dma((NG, 2)), dma((NG, 2)), dma((NG, 2)), dma((NG, 2)), dma((4,)), dma((4,)),
            dma((O, 2 * NP)), dma((O, 2 * NP)), dma((O, 2 * NP)), dma((O, 2 * NP)),
        ],
        compiler_params=pltpu.CompilerParams(
            collective_id=0, has_side_effects=True, vmem_limit_bytes=48 * 2**20
        ),
        name="packed_cycle",
    )(occ_irreps, vir_irreps.reshape(V // BV, BV), amplitudes, w_ovvo)


def shards(amplitudes, w_ovvo, occ_irreps, vir_irreps):
    result, fits = packed(amplitudes, w_ovvo, occ_irreps, vir_irreps)
    return lax.cond(
        fits[0] == 1,
        lambda: result,
        lambda: general(amplitudes, w_ovvo, occ_irreps, vir_irreps)[:, None],
    )


def solution(mesh):
    in_specs = (P(None, "pair", None, "virt"), P("pair", "virt", None), P(), P())
    out_specs = P(None, "pair", None, "virt")
    return jax.shard_map(shards, mesh=mesh, in_specs=in_specs, out_specs=out_specs, check_vma=False)
```
